256 devices in a mesh: seq: 256 (over x, y, z, core).
Axes of the slice: x: 4, y: 4, z: 8, core: 2. Of those that a mesh axis runs over, the one named last changes fastest.
Arguments:
- queries: bfloat16 [40960, 1024], P('seq'), may hold values from -8 to 8
- key_rows: bfloat16 [40960, 1024], P('seq'), may hold values from -8 to 8
- value_rows: bfloat16 [40960, 1024], P('seq'), may hold values from -6 to 6
- out_weight: bfloat16 [1048576], P('seq'), may hold values from -0.75 to 0.75
- cotangent: bfloat16 [40960, 1024], P('seq'), may hold values from -6 to 6
- row_lengths: int32 [204], replicated, may hold values from 1 to 400, 40960 in all
- window_shift: int32 [40960], P('seq'), may hold values from 0 to 720
Outputs:
- layer_out: bfloat16 [40960, 1024], P('seq')
- grad_queries: bfloat16 [40960, 1024], P('seq')
- grad_keys: bfloat16 [40960, 1024], P('seq')
- grad_values: bfloat16 [40960, 1024], P('seq')
- grad_weight: float32 [1048576], P('seq')
The draws below stay inside these ranges and needn't reach their ends.
All inputs are finite; a program needn't handle non-finite values.
Results may differ from the reference program's by a relative error of at most 0.025.
Values may be sent and summed in bfloat16 or wider, within the bound.
A program may use at most 128 MiB of HBM per device.

```python
import math
import jax
import jax.numpy as jnp
import numpy as np
from jax import lax

D = 1024
HEADS = 16
HEAD = 64
WIN = 1120
MOSTROW = 400
PTS_DEV = 160
NPTS = 40960
ROWS = 204
HALO_DEV = 7


def draw_queries(key, part):
    noise_key = jax.random.fold_in(key, 17)
    result = jnp.clip(2.0 * jax.random.normal(noise_key, (NPTS, D), jnp.float32), -8.0, 8.0)
    return result.astype(jnp.bfloat16)


def draw_key_rows(key, part):
    noise_key = jax.random.fold_in(key, 29)
    result = jnp.clip(jax.random.normal(noise_key, (NPTS, D), jnp.float32), -8.0, 8.0)
    return result.astype(jnp.bfloat16)


def set_ends(array, key, least, high):
    longest = array.shape.index(max(array.shape))
    spots = []
    for shift in (0, 1):
        where = [jax.random.randint(jax.random.fold_in(key, axis), (), 0, length) for axis, length in enumerate(array.shape)]
        where[longest] = (where[longest] + shift) % array.shape[longest]
        spots.append(tuple(where))
    return array.at[spots[0]].set(least).at[spots[1]].set(high)


def levels(rng, shape, pieces, low, high):
    def one(dim, shards_of):
        draws = jax.random.uniform(jax.random.fold_in(jax.random.fold_in(rng, 6), dim), (shards_of,), jnp.float32, low / len(pieces), high / len(pieces))
        return jnp.repeat(jnp.exp(draws), shape[dim] // shards_of).reshape((-1,) + (1,) * (len(shape) - dim - 1))

    level = one(*pieces[0])
    for cut in pieces[1:]:
        level = level * one(*cut)
    return level


def profile(amount, total, limit, lean):
    weights = [(1 << 20) // math.isqrt(rank ** lean) + 1 for rank in range(2, amount + 1)]
    rest, given = total - limit - (amount - 1), [1] * (amount - 1)
    while rest > 0:
        movable = [i for i in range(amount - 1) if given[i] < limit]
        pool, left = sum([weights[i] for i in movable]), rest
        for i in movable:
            more = min(limit - given[i], max(1, left * weights[i] // pool), rest)
            given[i] = given[i] + more
            rest = rest - more
    return np.array([limit] + given)


def ragged(key, number_of, total, limit, slope):
    if number_of == 2:
        one = jax.random.randint(key, (), max(1, total - limit), min(limit, total - 1) + 1)
        return jnp.stack([one, total - one])
    tallies = jnp.asarray(profile(number_of, total, limit, slope), jnp.int32)
    twos = (number_of - 1) // 2
    donor, receiver = tallies[1:1 + 2 * twos:2], tallies[2:2 + 2 * twos:2]
    room = jnp.minimum(donor - 1, limit - receiver)
    moved = jax.random.randint(jax.random.fold_in(key, 1), (twos,), 0, 1 << 20) % (room + 1)
    tallies = tallies.at[1:1 + 2 * twos:2].set(donor - moved).at[2:2 + 2 * twos:2].set(receiver + moved)
    return tallies[jax.random.permutation(jax.random.fold_in(key, 2), number_of)]


def normal_values(stream_key, dims, width, reach, cuts=(), kind=jnp.bfloat16):
    drawn = width * jax.random.normal(stream_key, dims, jnp.float32)
    if cuts:
        drawn = drawn * levels(stream_key, dims, cuts, -0.22, 0.18)
    return jnp.clip(drawn, -reach, reach).astype(kind)


def setup_inputs(seed: int = 0) -> dict:
    key_list = jax.random.split(jax.random.key(seed), 8)
    queries = draw_queries(jax.random.fold_in(key_list[7], 71), 0)
    key_rows = draw_key_rows(jax.random.fold_in(key_list[7], 71), 0)
    value_rows = normal_values(key_list[2], (NPTS, D), 1.0, 6.0, ((0, 256),))
    out_weight = normal_values(key_list[3], (D * D,), (4.0 / D ** 0.5), 0.75, ((0, 256),))
    cotangent = normal_values(key_list[4], (NPTS, D), 1.0, 6.0, ((0, 256),))
    row_lengths = ragged(key_list[5], ROWS, NPTS, MOSTROW, 1).astype(jnp.int32)
    window_shift = set_ends(jax.random.randint(key_list[6], (NPTS,), 0, WIN - MOSTROW + 1), jax.random.fold_in(key_list[6], 1), 0, WIN - MOSTROW).astype(jnp.int32)
    return dict(queries=queries, key_rows=key_rows, value_rows=value_rows, out_weight=out_weight, cotangent=cotangent, row_lengths=row_lengths, window_shift=window_shift)


def head_view(block):
    return block.reshape(block.shape[0], HEADS, HEAD).astype(jnp.float32)


def window_starts(row_lengths, window_shift, first_point, all_points):
    point_index = first_point + jnp.arange(window_shift.shape[0], dtype=jnp.int32)
    row_ends = jnp.cumsum(row_lengths).astype(jnp.int32)
    passed = row_ends[None, :] <= point_index[:, None]
    row_first = jnp.sum(jnp.where(passed, row_lengths[None, :], 0), axis=1).astype(jnp.int32)
    return jnp.clip(row_first - window_shift, 0, all_points - WIN).astype(jnp.int32)


def reference(queries, key_rows, value_rows, out_weight, cotangent, row_lengths, window_shift):
    head_scale = 1.0 / (HEAD ** 0.5)
    margin = PTS_DEV * HALO_DEV
    rim_rows = (2 * HALO_DEV + 1) * PTS_DEV
    starts = window_starts(row_lengths, window_shift, 0, NPTS)
    keys_padded = jnp.pad(key_rows, ((margin, margin), (0, 0)))
    values_padded = jnp.pad(value_rows, ((margin, margin), (0, 0)))
    block_list = jnp.arange(NPTS // PTS_DEV, dtype=jnp.int32)

    def block_scores(block_index):
        first_point = (block_index * PTS_DEV).astype(jnp.int32)
        query_block = lax.dynamic_slice_in_dim(queries, first_point, PTS_DEV, 0)
        key_block = lax.dynamic_slice_in_dim(keys_padded, first_point, rim_rows, 0)
        start_block = lax.dynamic_slice_in_dim(starts, first_point, PTS_DEV, 0)
        key_index = first_point - margin + jnp.arange(rim_rows, dtype=jnp.int32)
        allowed = (key_index[None, :] >= start_block[:, None]) & (key_index[None, :] < start_block[:, None] + WIN)
        scores = jnp.einsum("qhd,khd->hqk", head_view(query_block), head_view(key_block)) * head_scale
        return jnp.where(allowed[None], scores, -jnp.inf)

    def forward_block(block_index):
        first_point = (block_index * PTS_DEV).astype(jnp.int32)
        scores = block_scores(block_index)
        value_block = head_view(lax.dynamic_slice_in_dim(values_padded, first_point, rim_rows, 0))
        row_top = jnp.max(scores, axis=2, keepdims=True)
        log_total = row_top + jnp.log(jnp.sum(jnp.exp(scores - row_top), axis=2, keepdims=True))
        softmax_out = lax.optimization_barrier(jnp.exp(scores - log_total).astype(jnp.bfloat16))
        mixed = jnp.einsum("hqk,khd->qhd", softmax_out.astype(jnp.float32), value_block)
        return mixed.reshape(PTS_DEV, D).astype(jnp.bfloat16), log_total[:, :, 0].T

    mixed, log_total = lax.map(forward_block, block_list)
    mixed = mixed.reshape(NPTS, D)
    log_total = log_total.reshape(NPTS, HEADS)
    square = out_weight.reshape(D, D)
    layer_out = jnp.dot(mixed, square, preferred_element_type=jnp.float32).astype(jnp.bfloat16)
    grad_mixed = jnp.dot(cotangent, square.T, preferred_element_type=jnp.float32).astype(jnp.bfloat16)
    grad_weight = (jnp.dot(mixed.T, cotangent, preferred_element_type=jnp.float32) * (1.0 / (NPTS ** 0.5))).reshape(D * D)
    row_delta = jnp.sum((grad_mixed.astype(jnp.float32) * mixed.astype(jnp.float32)).reshape(NPTS, HEADS, HEAD), axis=2)

    def backward_block(carry, block_index):
        keys_sum, values_sum = carry
        first_point = (block_index * PTS_DEV).astype(jnp.int32)
        scores = block_scores(block_index)
        query_block = head_view(lax.dynamic_slice_in_dim(queries, first_point, PTS_DEV, 0))
        key_block = head_view(lax.dynamic_slice_in_dim(keys_padded, first_point, rim_rows, 0))
        value_block = head_view(lax.dynamic_slice_in_dim(values_padded, first_point, rim_rows, 0))
        grad_block = head_view(lax.dynamic_slice_in_dim(grad_mixed, first_point, PTS_DEV, 0))
        total_block = lax.dynamic_slice_in_dim(log_total, first_point, PTS_DEV, 0).T[:, :, None]
        delta_block = lax.dynamic_slice_in_dim(row_delta, first_point, PTS_DEV, 0).T[:, :, None]
        chances = jnp.exp(scores - total_block)
        grad_scores = jnp.einsum("qhd,khd->hqk", grad_block, value_block)
        slopes = lax.optimization_barrier((chances * (grad_scores - delta_block)).astype(jnp.bfloat16)).astype(jnp.float32)
        rounded = lax.optimization_barrier(chances.astype(jnp.bfloat16)).astype(jnp.float32)
        grad_query = (jnp.einsum("hqk,khd->qhd", slopes, key_block) * head_scale).reshape(PTS_DEV, D).astype(jnp.bfloat16)
        key_part = jnp.einsum("hqk,qhd->khd", slopes, query_block).reshape(rim_rows, D)
        value_part = jnp.einsum("hqk,qhd->khd", rounded, grad_block).reshape(rim_rows, D)
        keys_sum = lax.dynamic_update_slice_in_dim(keys_sum, lax.dynamic_slice_in_dim(keys_sum, first_point, rim_rows, 0) + key_part, first_point, 0)
        values_sum = lax.dynamic_update_slice_in_dim(values_sum, lax.dynamic_slice_in_dim(values_sum, first_point, rim_rows, 0) + value_part, first_point, 0)
        return (keys_sum, values_sum), grad_query

    zeros_pad = jnp.zeros((NPTS + 2 * margin, D), jnp.float32)
    (keys_sum, values_sum), grad_queries = lax.scan(backward_block, (zeros_pad, zeros_pad), block_list)
    grad_queries = grad_queries.reshape(NPTS, D)
    grad_keys = (keys_sum[margin:margin + NPTS] * head_scale).astype(jnp.bfloat16)
    grad_values = values_sum[margin:margin + NPTS].astype(jnp.bfloat16)
    return layer_out, grad_queries, grad_keys, grad_values, grad_weight
```

```python
import functools
import math

import jax
import jax.numpy as jnp
from jax import lax
from jax.experimental import pallas as pl
from jax.experimental.pallas import tpu as pltpu
from jax.sharding import PartitionSpec as P

D = 1024
HEADS = 16
HEAD = 64
WIN = 1120
RIM = 1120
TQ = 128
SPAN = 2432
FAR = -1e30
MESH = pl.DeviceIdType.MESH
BF16 = jnp.bfloat16
F32 = jnp.float32
VMEM_LIMIT = 56 * 1024 * 1024


def spot():
    me = lax.axis_index("seq")
    return me, me // HEADS, lax.rem(me, HEADS)


def push(src, dst, send, recv, device):
    return pltpu.make_async_remote_copy(
        src_ref=src, dst_ref=dst, send_sem=send, recv_sem=recv, device_id=(device,), device_id_type=MESH
    )


def meet(devices):
    barrier = pltpu.get_barrier_semaphore()
    for device in devices:
        pl.semaphore_signal(barrier, inc=1, device_id=(device,), device_id_type=MESH)
    pl.semaphore_wait(barrier, len(devices))


def lanes_low(shape):
    return lax.broadcasted_iota(jnp.int32, shape, 1) < HEAD


def pair_up(left, right, out, points):
    for k in range(HEADS // 2):
        cols = pl.ds(2 * HEAD * k, 2 * HEAD)
        a, b = left[:, cols], right[:, cols]
        out[2 * k] = jnp.concatenate([a[:, :HEAD], b[:, :HEAD]], axis=1)
        out[2 * k + 1] = jnp.concatenate([a[:, HEAD:], b[:, HEAD:]], axis=1)


def split_up(blocks, left, right):
    for k in range(HEADS // 2):
        cols = pl.ds(2 * HEAD * k, 2 * HEAD)
        a, b = blocks[2 * k], blocks[2 * k + 1]
        left[:, cols] = jnp.concatenate([a[:, :HEAD], b[:, :HEAD]], axis=1)
        right[:, cols] = jnp.concatenate([a[:, HEAD:], b[:, HEAD:]], axis=1)


def gather_kernel(
    rows,
    q_ref, k_ref, v_ref, cot_ref, w_ref, st_ref,
    kv_ref, qg_ref, starts_ref, weight_ref,
    kv_send, qg_send, st_recv, w_recv, w_wide, grad,
    kv_ss, kv_rs, qg_ss, qg_rs, st_ss, st_rs, w_ss, w_rs, x_ss, x_rs, s_ss, s_rs, rim_ss, rim_rs,
):
    me, row, place = spot()
    core = lax.rem(me, 2)
    points = q_ref.shape[0]
    span = HEADS * points
    sibling = me + 1 - 2 * core
    mates = [row * HEADS + lax.rem(place + i, HEADS) for i in range(1, HEADS)]
    peers = [lax.rem(row + i, rows) * HEADS + place for i in range(1, rows)]
    lower = lax.rem(row + rows - 1, rows) * HEADS + place
    upper = lax.rem(row + 1, rows) * HEADS + place
    meet(mates + peers)

    live = []

    def go(copy):
        copy.start()
        live.append(copy)
        return copy

    part = w_ref.shape[0]
    w_copies = [
        go(push(w_ref, w_recv.at[pl.ds(place * part, part)], w_ss.at[i], w_rs.at[i], mates[i]))
        for i in range(HEADS - 1)
    ]
    w_recv[pl.ds(pl.multiple_of(place * part, part), part)] = w_ref[...]
    st_copies = [
        go(push(st_ref, st_recv.at[place], st_ss.at[i], st_rs.at[i], mates[i])) for i in range(HEADS - 1)
    ]
    st_recv[place] = st_ref[...]

    pair_up(k_ref, v_ref, kv_send, points)
    mine = pl.ds(pl.multiple_of(RIM + place * points, 16), points)
    kv_copies = [
        go(push(kv_send.at[lax.rem(place + i + 1, HEADS)], kv_ref.at[mine], kv_ss.at[i], kv_rs.at[i], mates[i]))
        for i in range(HEADS - 1)
    ]
    kv_ref[mine] = kv_send[place]
    tail = kv_ref.shape[0] - (2 * RIM + span)
    kv_ref[pl.ds(2 * RIM + span, tail)] = jnp.zeros((tail, 2 * HEAD), BF16)

    for copy in w_copies:
        copy.wait_recv()
    w_wide[...] = w_recv[...].astype(F32)
    wrows = HEADS * part * 2 * HEAD // D
    half = wrows // 2
    own = pl.multiple_of(row * wrows, 16)
    for b in range(D // 128):
        weight_ref[pl.ds(own, wrows), pl.ds(b * 128, 128)] = w_wide[pl.ds(b, wrows, stride=D // 128), :].astype(BF16)
    my_half = weight_ref.at[pl.ds(pl.multiple_of(own + core * half, 16), half)]
    x_copies = [go(push(my_half, my_half, x_ss.at[i], x_rs.at[i], peers[i])) for i in range(rows - 1)]

    for copy in kv_copies:
        copy.wait_recv()
    rim_copies = [
        go(push(kv_ref.at[pl.ds(RIM, RIM)], kv_ref.at[pl.ds(RIM + span, RIM)], rim_ss.at[0], rim_rs.at[0], lower)),
        go(push(kv_ref.at[pl.ds(span, RIM)], kv_ref.at[pl.ds(0, RIM)], rim_ss.at[1], rim_rs.at[1], upper)),
    ]

    s_copies = []
    for i in range(rows - 1):
        x_copies[i].wait_recv()
        source = lax.rem(row + rows - i - 1, rows)
        came = weight_ref.at[pl.ds(pl.multiple_of(source * wrows + core * half, 16), half)]
        s_copies.append(go(push(came, came, s_ss.at[i], s_rs.at[i], sibling)))
    for copy in s_copies:
        copy.wait_recv()

    grad[...] = lax.dot_general(
        cot_ref[...], weight_ref[...], (((1,), (1,)), ((), ())), preferred_element_type=F32
    ).astype(BF16)
    pair_up(q_ref, grad, qg_send, points)
    here = pl.ds(pl.multiple_of(place * points, 16), points)
    qg_copies = [
        go(push(qg_send.at[lax.rem(place + i + 1, HEADS)], qg_ref.at[here], qg_ss.at[i], qg_rs.at[i], mates[i]))
        for i in range(HEADS - 1)
    ]
    qg_ref[here] = qg_send[place]

    for copy in st_copies:
        copy.wait_recv()
    for t in range(span // TQ):
        total = None
        for p in range(HEADS):
            first = p * points // TQ
            if first <= t <= first + 1:
                piece = st_recv[p, 0:1, pl.ds((t - first) * TQ, TQ)]
                total = piece if total is None else total + piece
        starts_ref[t : t + 1, :] = total

    for copy in rim_copies:
        copy.wait_recv()
    for copy in qg_copies:
        copy.wait_recv()
    for copy in live:
        copy.wait_send()


def attend_kernel(kv_ref, qg_ref, starts_ref, base_ref, oq_ref, dkv_ref, kvt, acc, scores, slants, pairs):
    low = lanes_low((TQ, 2 * HEAD))
    scale = 1.0 / math.sqrt(HEAD)
    fold = scale * math.log2(math.e)
    chunks = [(k, min(256, SPAN - k)) for k in range(0, SPAN, 256)]

    @pl.loop(0, kv_ref.shape[0] // 128)
    def _(t):
        at = pl.ds(pl.multiple_of(t * 128, 128), 128)
        kvt[:, at] = kv_ref[at, :].astype(F32).T.astype(BF16)
        acc[at, :] = jnp.zeros((128, 2 * HEAD), F32)

    @pl.loop(0, qg_ref.shape[0] // TQ)
    def _(t):
        first = pl.multiple_of(t * TQ, TQ)
        qg = qg_ref[pl.ds(first, TQ), :]
        zero = jnp.zeros_like(qg)
        both = jnp.concatenate([jnp.where(low, qg, zero), jnp.where(low, zero, qg)], axis=0)
        rel = starts_ref[pl.ds(t, 1), :] - base_ref[0] - first
        top = jnp.full((8, TQ), FAR, F32)
        for k, n in chunks:
            made = lax.dot_general(
                kv_ref[pl.ds(first + k, n), :], both, (((1,), (1,)), ((), ())), preferred_element_type=F32
            )
            past = lax.broadcasted_iota(jnp.int32, (n, TQ), 0) - (rel - k)
            s = jnp.where((past >= 0) & (past < WIN), made[:, :TQ] * fold, FAR)
            scores[pl.ds(k, n), :] = s
            slants[pl.ds(k, n), :] = made[:, TQ:]
            top = jnp.maximum(top, jnp.max(s.reshape(n // 8, 8, TQ), axis=0))
        top = jnp.max(top, axis=0, keepdims=True)
        total = jnp.zeros((8, TQ), F32)
        cross = jnp.zeros((8, TQ), F32)
        out_t = jnp.zeros((HEAD, TQ), F32)
        for k, n in chunks:
            p = jnp.exp2(scores[pl.ds(k, n), :] - top)
            total += jnp.sum(p.reshape(n // 8, 8, TQ), axis=0)
            cross += jnp.sum((p * slants[pl.ds(k, n), :]).reshape(n // 8, 8, TQ), axis=0)
            p = p.astype(BF16)
            pairs[pl.ds(k, n), TQ:] = p
            out_t += jnp.dot(kvt[HEAD:, pl.ds(first + k, n)], p, preferred_element_type=F32)
        share = 1.0 / jnp.sum(total, axis=0, keepdims=True)
        delta = jnp.sum(cross, axis=0, keepdims=True) * share
        by_row = jnp.broadcast_to(share, (TQ, TQ)).T
        scaled = qg.astype(F32) * by_row
        scaled = jnp.concatenate(
            [jnp.where(low, scaled * scale, 0.0), jnp.where(low, 0.0, scaled)], axis=0
        ).astype(BF16)
        dq_t = jnp.zeros((HEAD, TQ), F32)
        for k, n in chunks:
            p = pairs[pl.ds(k, n), TQ:].astype(F32)
            ds = (p * (slants[pl.ds(k, n), :] - delta)).astype(BF16)
            pairs[pl.ds(k, n), :TQ] = ds
            dq_t += jnp.dot(kvt[:HEAD, pl.ds(first + k, n)], ds, preferred_element_type=F32)
            acc[pl.ds(first + k, n), :] += jnp.dot(pairs[pl.ds(k, n), :], scaled, preferred_element_type=F32)
        back = jnp.concatenate([dq_t * (share * scale), out_t * share], axis=0)
        oq_ref[pl.ds(first, TQ), :] = back.T.astype(BF16)

    @pl.loop(0, kv_ref.shape[0] // 128)
    def _(t):
        at = pl.ds(pl.multiple_of(t * 128, 128), 128)
        dkv_ref[at, :] = acc[at, :].astype(BF16)


def scatter_kernel(
    rows, inverse_root,
    oq_ref, dkv_ref, cot_ref, weight_ref,
    out_ref, dq_ref, dk_ref, dv_ref, dw_ref,
    oq_recv, kv_recv, rim_recv, kv_sum, mixed, terms, sib_recv, half_sum, peer_recv, flat, last_recv,
    oq_ss, oq_rs, kv_ss, kv_rs, rim_ss, rim_rs, s_ss, s_rs, x_ss, x_rs, z_ss, z_rs,
):
    me, row, place = spot()
    core = lax.rem(me, 2)
    points = cot_ref.shape[0]
    span = HEADS * points
    sibling = me + 1 - 2 * core
    mates = [row * HEADS + lax.rem(place + i, HEADS) for i in range(1, HEADS)]
    peers = [lax.rem(row + i, rows) * HEADS + place for i in range(1, rows)]
    lower = lax.rem(row + rows - 1, rows) * HEADS + place
    upper = lax.rem(row + 1, rows) * HEADS + place
    meet(mates + peers)

    live = []

    def go(copy):
        copy.start()
        live.append(copy)
        return copy

    def block(at, offset=0):
        return pl.ds(pl.multiple_of(offset + at * points, 16), points)

    oq_copies = [
        go(push(oq_ref.at[block(lax.rem(place + i + 1, HEADS))], oq_recv.at[place], oq_ss.at[i], oq_rs.at[i], mates[i]))
        for i in range(HEADS - 1)
    ]
    oq_recv[place] = oq_ref[block(place), :]
    rim_copies = [
        go(push(dkv_ref.at[pl.ds(0, RIM)], rim_recv.at[1], rim_ss.at[0], rim_rs.at[0], lower)),
        go(push(dkv_ref.at[pl.ds(RIM + span, RIM)], rim_recv.at[0], rim_ss.at[1], rim_rs.at[1], upper)),
    ]
    for copy in rim_copies:
        copy.wait_recv()
    kv_sum[pl.ds(0, RIM), :] = (dkv_ref[pl.ds(RIM, RIM), :].astype(F32) + rim_recv[0].astype(F32)).astype(BF16)
    kv_sum[pl.ds(RIM, span - 2 * RIM), :] = dkv_ref[pl.ds(2 * RIM, span - 2 * RIM), :]
    kv_sum[pl.ds(span - RIM, RIM), :] = (dkv_ref[pl.ds(span, RIM), :].astype(F32) + rim_recv[1].astype(F32)).astype(BF16)
    kv_copies = [
        go(push(kv_sum.at[block(lax.rem(place + i + 1, HEADS))], kv_recv.at[place], kv_ss.at[i], kv_rs.at[i], mates[i]))
        for i in range(HEADS - 1)
    ]
    kv_recv[place] = kv_sum[block(place), :]

    for copy in oq_copies:
        copy.wait_recv()
    split_up(oq_recv, dq_ref, mixed)

    half = HEAD // 2
    for k in range(HEADS // 2):
        term = lax.dot_general(
            mixed[:, pl.ds(2 * HEAD * k, 2 * HEAD)], cot_ref[...], (((0,), (0,)), ((), ())), preferred_element_type=F32
        ).astype(BF16)
        for j in range(4):
            terms[j % 2, pl.ds((2 * k + j // 2) * half, half), :] = term[j * half : (j + 1) * half]
    s_copy = go(push(terms.at[1 - core], sib_recv, s_ss, s_rs, sibling))
    out_ref[...] = jnp.dot(mixed[...], weight_ref[...], preferred_element_type=F32).astype(BF16)
    s_copy.wait_recv()

    def to_sum(r):
        return pl.ds(pl.multiple_of(r * half, half), half)

    x_copies = []
    for i in list(range(1, rows)) + [0]:
        at = to_sum(lax.rem(row + i, rows))
        half_sum[at, :] = (terms[core, at, :].astype(F32) + sib_recv[at, :].astype(F32)).astype(BF16)
        if i:
            x_copies.append(
                go(push(half_sum.at[at], peer_recv.at[i - 1], x_ss.at[i - 1], x_rs.at[i - 1], peers[i - 1]))
            )
    total = half_sum[to_sum(row), :].astype(F32)
    for i in range(rows - 1):
        x_copies[i].wait_recv()
        total += peer_recv[i].astype(F32)
    total = total * inverse_root
    for b in range(D // 128):
        flat[pl.ds(b, half, stride=D // 128), :] = total[:, b * 128 : (b + 1) * 128]

    own = place // 2
    part = dw_ref.shape[0]
    z_copies = []
    for j in range(HEADS // 2):
        goal = core * (HEADS // 2) + j
        piece = flat.at[pl.ds(j * part, part)]
        copy = push(piece, last_recv.at[own], z_ss.at[j], z_rs.at[own], row * HEADS + goal)

        @pl.when(goal != place)
        def _():
            copy.start()

        @pl.when(goal == place)
        def _():
            last_recv[own] = flat[pl.ds(j * part, part), :]

        z_copies.append((goal, copy))

    for copy in kv_copies:
        copy.wait_recv()
    split_up(kv_recv, dk_ref, dv_ref)

    for z in range(HEADS // 2):
        source = 2 * z + place // (HEADS // 2)

        @pl.when(source != place)
        def _():
            push(flat.at[pl.ds(0, part)], last_recv.at[z], z_ss.at[0], z_rs.at[z], row * HEADS + source).wait_recv()

    dw_ref[...] = jnp.sum(last_recv[...], axis=0)
    for goal, copy in z_copies:

        @pl.when(goal != place)
        def _():
            copy.wait_send()

    for copy in live:
        copy.wait_send()


def window_starts(row_lengths, window_shift, first_point, all_points):
    count = row_lengths.shape[0]
    order = jnp.arange(count, dtype=jnp.int32)
    ends = jnp.sum(jnp.where(order[:, None] <= order[None, :], row_lengths[:, None], 0), axis=0)
    index = first_point + jnp.arange(window_shift.shape[0], dtype=jnp.int32)
    passed = ends[None, :] <= index[:, None]
    row_first = jnp.sum(jnp.where(passed, row_lengths[None, :], 0), axis=1)
    return jnp.clip(row_first - window_shift, 0, all_points - WIN)


def in_vmem(count):
    return [pl.BlockSpec(memory_space=pltpu.VMEM)] * count


def per_device(queries, key_rows, value_rows, out_weight, cotangent, row_lengths, window_shift):
    points = queries.shape[0]
    devices = lax.axis_size("seq")
    rows = devices // HEADS
    span = HEADS * points
    held = span - TQ + SPAN
    me = lax.axis_index("seq")
    starts = window_starts(row_lengths, window_shift, me * points, devices * points)
    offset = lax.rem(lax.rem(me, HEADS) * points, TQ)
    starts = lax.dynamic_update_slice(jnp.zeros((1, 2 * TQ), jnp.int32), starts[None, :], (0, offset))
    starts = jnp.concatenate([starts, jnp.zeros((7, 2 * TQ), jnp.int32)], axis=0)
    w_part = out_weight.shape[0] // 128
    wide = 2 * HEAD
    dma = pltpu.SemaphoreType.DMA
    ring, cross = dma((HEADS - 1,)), dma((rows - 1,))

    kv, qg, row_starts, weight = pl.pallas_call(
        functools.partial(gather_kernel, rows),
        out_shape=(
            jax.ShapeDtypeStruct((held, wide), BF16),
            jax.ShapeDtypeStruct((span, wide), BF16),
            jax.ShapeDtypeStruct((span // TQ, TQ), jnp.int32),
            jax.ShapeDtypeStruct((D, D), BF16),
        ),
        in_specs=in_vmem(6),
        out_specs=tuple(in_vmem(4)),
        scratch_shapes=[
            pltpu.VMEM((HEADS, points, wide), BF16),
            pltpu.VMEM((HEADS, points, wide), BF16),
            pltpu.VMEM((HEADS, 8, 2 * TQ), jnp.int32),
            pltpu.VMEM((HEADS * w_part, 128), BF16),
            pltpu.VMEM((HEADS * w_part, 128), F32),
            pltpu.VMEM((points, D), BF16),
            ring, ring, ring, ring, ring, ring, ring, ring, cross, cross, cross, cross, dma((2,)), dma((2,)),
        ],
        compiler_params=pltpu.CompilerParams(
            collective_id=0, has_side_effects=True, vmem_limit_bytes=VMEM_LIMIT
        ),
        name="gather_heads",
    )(queries, key_rows, value_rows, cotangent, out_weight.reshape(w_part, 128), starts)

    base = (me // HEADS * span - RIM).reshape(1)
    oq, dkv = pl.pallas_call(
        attend_kernel,
        out_shape=(jax.ShapeDtypeStruct((span, wide), BF16), jax.ShapeDtypeStruct((held, wide), BF16)),
        in_specs=in_vmem(3) + [pl.BlockSpec(memory_space=pltpu.SMEM)],
        out_specs=tuple(in_vmem(2)),
        scratch_shapes=[
            pltpu.VMEM((wide, held), BF16),
            pltpu.VMEM((held, wide), F32),
            pltpu.VMEM((SPAN, TQ), F32),
            pltpu.VMEM((SPAN, TQ), F32),
            pltpu.VMEM((SPAN, 2 * TQ), BF16),
        ],
        compiler_params=pltpu.CompilerParams(vmem_limit_bytes=VMEM_LIMIT),
        name="attend",
    )(kv, qg, row_starts, base)

    half = HEAD // 2
    full = jax.ShapeDtypeStruct((points, D), BF16)
    out, dq, dk, dv, dw = pl.pallas_call(
        functools.partial(scatter_kernel, rows, 1.0 / math.sqrt(devices * points)),
        out_shape=(full, full, full, full, jax.ShapeDtypeStruct((w_part, 128), F32)),
        in_specs=in_vmem(4),
        out_specs=tuple(in_vmem(5)),
        scratch_shapes=[
            pltpu.VMEM((HEADS, points, wide), BF16),
            pltpu.VMEM((HEADS, points, wide), BF16),
            pltpu.VMEM((2, RIM, wide), BF16),
            pltpu.VMEM((span, wide), BF16),
            pltpu.VMEM((points, D), BF16),
            pltpu.VMEM((2, HEADS * half, D), BF16),
            pltpu.VMEM((HEADS * half, D), BF16),
            pltpu.VMEM((HEADS * half, D), BF16),
            pltpu.VMEM((rows - 1, half, D), BF16),
            pltpu.VMEM((half * D // 128, 128), F32),
            pltpu.VMEM((HEADS // 2, w_part, 128), F32),
            ring, ring, ring, ring, dma((2,)), dma((2,)), dma, dma, cross, cross,
            dma((HEADS // 2,)), dma((HEADS // 2,)),
        ],
        compiler_params=pltpu.CompilerParams(
            collective_id=1, has_side_effects=True, vmem_limit_bytes=VMEM_LIMIT
        ),
        name="scatter_heads",
    )(oq, dkv, cotangent, weight)
    return (out, dq, dk, dv, dw.reshape(-1))


def solution(mesh):
    whole = P("seq", None)
    return jax.shard_map(
        per_device,
        mesh=mesh,
        in_specs=(whole, whole, whole, P("seq"), whole, P(), P("seq")),
        out_specs=(whole, whole, whole, whole, P("seq")),
        check_vma=False,
    )
```

```python
import functools
import math

import jax
import jax.numpy as jnp
from jax import lax
from jax.experimental import pallas as pl
from jax.experimental.pallas import tpu as pltpu
from jax.sharding import PartitionSpec as P

D = 1024
HEADS = 16
HEAD = 64
WIN = 1120
RIM = 1120
TQ = 256
SPAN = 2496
CHUNKS = [(k, min(256, SPAN - k)) for k in range(0, SPAN, 256)]
FAR = -1e30
MESH = pl.DeviceIdType.MESH
BF16 = jnp.bfloat16
F32 = jnp.float32
VMEM_LIMIT = 56 * 1024 * 1024


def spot():
    me = lax.axis_index("seq")
    return me, me // HEADS, lax.rem(me, HEADS)


def push(src, dst, send, recv, device):
    return pltpu.make_async_remote_copy(
        src_ref=src, dst_ref=dst, send_sem=send, recv_sem=recv, device_id=(device,), device_id_type=MESH
    )


def lanes_low(shape):
    return lax.broadcasted_iota(jnp.int32, shape, 1) < HEAD


def pair_up(left, right, out):
    for k in range(HEADS // 2):
        cols = pl.ds(2 * HEAD * k, 2 * HEAD)
        a, b = left[:, cols], right[:, cols]
        out[2 * k] = jnp.concatenate([a[:, :HEAD], b[:, :HEAD]], axis=1)
        out[2 * k + 1] = jnp.concatenate([a[:, HEAD:], b[:, HEAD:]], axis=1)


def split_up(blocks, left, right):
    for k in range(HEADS // 2):
        cols = pl.ds(2 * HEAD * k, 2 * HEAD)
        a, b = blocks[2 * k], blocks[2 * k + 1]
        left[:, cols] = jnp.concatenate([a[:, :HEAD], b[:, :HEAD]], axis=1)
        right[:, cols] = jnp.concatenate([a[:, HEAD:], b[:, HEAD:]], axis=1)


def halves(ref):
    half = ref.shape[0] // 2
    return ref.at[pl.ds(0, half)], ref.at[pl.ds(half, half)]


def own_starts(len_ref, shift_ref, first_point, offset, all_points):
    count, points = len_ref.shape[1], shift_ref.shape[1]
    lens = jnp.concatenate([len_ref[...], jnp.zeros((1, 256 - count), jnp.int32)], axis=1)
    order = lax.broadcasted_iota(jnp.int32, (256, 256), 0)
    column = lax.broadcasted_iota(jnp.int32, (256, 256), 1)
    ends = jnp.sum(jnp.where(column <= order, lens, 0).astype(F32), axis=1, keepdims=True).astype(jnp.int32)
    lane = lax.broadcasted_iota(jnp.int32, (256, 256), 1)
    index = first_point + lane
    past = (ends <= index) & (order < count)
    row_first = jnp.max(jnp.where(past, jnp.broadcast_to(ends, (256, 256)), 0).astype(F32), axis=0, keepdims=True).astype(jnp.int32)
    shift = jnp.concatenate([shift_ref[...], jnp.zeros((1, 256 - points), jnp.int32)], axis=1)
    starts = jnp.clip(row_first - shift, 0, all_points - WIN)
    starts = jnp.where(lane[:1] < points, starts, 0)
    return pltpu.roll(jnp.broadcast_to(starts, (8, 256)), offset, 1)


def layer_kernel(
    rows, inverse_root,
    q_ref, k_ref, v_ref, cot_ref, w_ref, len_ref, shift_ref,
    out_ref, dq_recv, kv_back, dw_ref,
    kv_send, q_send, q_recv, g_send, g_recv, o_send, o_recv, dq_send,
    kv, qg, st_send, st_recv, starts, w_recv, w_wide, weight, grad,
    keys_t, values_t, acc, scores, probs, outs_t, shares, flows,
    mixed, terms, sib_recv, half_sum, peer_recv, flat, last_recv,
    rim_send, rim_recv, kv_sum,
    kv_ss, kv_rs, q_ss, q_rs, g_ss, g_rs, o_ss, o_rs, st_ss, st_rs, w_ss, w_rs,
    dq_ss, dq_rs, b_ss, b_rs, x_ss, x_rs, s_ss, s_rs, t_ss, t_rs, rim_ss, rim_rs, back_ss, back_rs, sib_ss, sib_rs,
    z_ss, z_rs,
):
    me, row, place = spot()
    core = lax.rem(me, 2)
    points = q_ref.shape[0]
    span = HEADS * points
    held = kv.shape[0]
    scale = 1.0 / math.sqrt(HEAD)
    fold = scale * math.log2(math.e)
    sibling = me + 1 - 2 * core
    near = range(HEADS - 1)
    far = range(rows - 1)
    goals = [lax.rem(place + i, HEADS) for i in range(1, HEADS)]
    mates = [row * HEADS + goal for goal in goals]
    peers = [lax.rem(row + i, rows) * HEADS + place for i in range(1, rows)]
    lower = lax.rem(row + rows - 1, rows) * HEADS + place
    upper = lax.rem(row + 1, rows) * HEADS + place

    def block(at, offset=0):
        return pl.ds(pl.multiple_of(offset + at * points, 16), points)

    barrier = pltpu.get_barrier_semaphore()
    for device in mates + peers:
        pl.semaphore_signal(barrier, inc=1, device_id=(device,), device_id_type=MESH)
    pair_up(k_ref, v_ref, kv_send)
    pair_up(*halves(q_ref), q_send)
    st_send[...] = own_starts(
        len_ref, shift_ref, me * points, lax.rem(place * points, 128), rows * span
    )
    pl.semaphore_wait(barrier, len(mates) + len(peers))

    part = w_ref.shape[0]
    w_at = pl.ds(pl.multiple_of(place * part, part), part)
    w_copies = [push(w_ref, w_recv.at[w_at], w_ss.at[i], w_rs.at[i], mates[i]) for i in near]
    kv_copies = [push(kv_send.at[goals[i]], kv.at[block(place, RIM)], kv_ss.at[i], kv_rs.at[i], mates[i]) for i in near]
    q_copies = [push(q_send.at[goals[i]], q_recv.at[place], q_ss.at[i], q_rs.at[i], mates[i]) for i in near]
    st_copies = [push(st_send, st_recv.at[place], st_ss.at[i], st_rs.at[i], mates[i]) for i in near]
    for copy in w_copies + kv_copies + st_copies + q_copies:
        copy.start()
    w_recv[w_at] = w_ref[...]
    kv[block(place, RIM), :] = kv_send[place]
    q_recv[place] = q_send[place]
    st_recv[place] = st_send[...]

    @pl.loop(0, held // 160)
    def _(t):
        acc[pl.ds(pl.multiple_of(t * 160, 160), 160), :] = jnp.zeros((160, 2 * HEAD), F32)

    values_t[HEAD:, :] = jnp.ones((16, values_t.shape[1]), BF16)

    for copy in w_copies:
        copy.wait_recv()
    w_wide[...] = w_recv[...].astype(F32)
    wrows = HEADS * part * 2 * HEAD // D
    half = wrows // 2
    own = pl.multiple_of(row * wrows, 16)
    for b in range(D // 128):
        weight[pl.ds(own, wrows), pl.ds(b * 128, 128)] = w_wide[pl.ds(b, wrows, stride=D // 128), :].astype(BF16)
    my_half = weight.at[pl.ds(pl.multiple_of(own + core * half, 16), half)]
    x_copies = [push(my_half, my_half, x_ss.at[i], x_rs.at[i], peers[i]) for i in far]
    for copy in x_copies:
        copy.start()

    for copy in kv_copies:
        copy.wait_recv()
    rim_copies = [
        push(kv.at[pl.ds(RIM, RIM)], kv.at[pl.ds(RIM + span, RIM)], rim_ss.at[0], rim_rs.at[0], lower),
        push(kv.at[pl.ds(span, RIM)], kv.at[pl.ds(0, RIM)], rim_ss.at[1], rim_rs.at[1], upper),
    ]
    for copy in rim_copies:
        copy.start()

    def turn(at, size):
        flipped = kv[pl.ds(at, size), :].astype(F32).T.astype(BF16)
        keys_t[:, pl.ds(at, size)] = flipped[:HEAD]
        values_t[:HEAD, pl.ds(at, size)] = flipped[HEAD:]

    inner = (-(-RIM // 128), (RIM + span) // 128)

    @pl.loop(*inner)
    def _(t):
        turn(pl.multiple_of(t * 128, 128), 128)

    t_copies = []
    for i in far:
        x_copies[i].wait_recv()
        source = lax.rem(row + rows - i - 1, rows)
        came = weight.at[pl.ds(pl.multiple_of(source * wrows + core * half, 16), half)]
        copy = push(came, came, t_ss.at[i], t_rs.at[i], sibling)
        copy.start()
        t_copies.append(copy)
    for copy in t_copies:
        copy.wait_recv()
    grad[...] = lax.dot_general(
        cot_ref[...], weight[...], (((1,), (1,)), ((), ())), preferred_element_type=F32
    ).astype(BF16)
    pair_up(*halves(grad), g_send)
    g_copies = [push(g_send.at[goals[i]], g_recv.at[place], g_ss.at[i], g_rs.at[i], mates[i]) for i in near]
    for copy in g_copies:
        copy.start()
    g_recv[place] = g_send[place]

    for copy in st_copies:
        copy.wait_recv()
    for t in range(span // 128):
        total = None
        for p in range(HEADS):
            first = p * points // 128
            if first <= t <= first + 1:
                piece = st_recv[p, 0:1, pl.ds((t - first) * 128, 128)]
                total = piece if total is None else total + piece
        starts[t // 2 : t // 2 + 1, (t % 2) * 128 : (t % 2 + 1) * 128] = total
    for copy in q_copies:
        copy.wait_recv()
    side = points // 2

    @pl.loop(0, HEADS)
    def _(p):
        a = q_recv[p]
        zero = jnp.zeros((side, HEAD), BF16)
        at = pl.multiple_of(p * points, 16)
        qg[pl.ds(at, side), :] = jnp.concatenate([a[:, :HEAD], zero], axis=1)
        qg[pl.ds(at + side, side), :] = jnp.concatenate([a[:, HEAD:], zero], axis=1)

    for copy in rim_copies:
        copy.wait_recv()

    @pl.loop(0, inner[0])
    def _(t):
        turn(pl.multiple_of(t * 128, 128), 128)

    @pl.loop(inner[1], held // 128)
    def _(t):
        turn(pl.multiple_of(t * 128, 128), 128)

    turn(held // 128 * 128, held % 128)

    base = row * span - RIM

    @pl.loop(0, span // TQ)
    def _(t):
        first = pl.multiple_of(t * TQ, TQ)
        query = qg[pl.ds(first, TQ), :]
        rel = starts[pl.ds(t, 1), :] - base - first
        top = jnp.full((8, TQ), FAR, F32)
        for k, n in CHUNKS:
            s = lax.dot_general(
                kv[pl.ds(first + k, n), :], query, (((1,), (1,)), ((), ())), preferred_element_type=F32
            )
            past = lax.broadcasted_iota(jnp.int32, (n, TQ), 0) - (rel - k)
            s = jnp.where((past >= 0) & (past < WIN), s, FAR)
            scores[pl.ds(k, n), :] = s
            top = jnp.maximum(top, jnp.max(s.reshape(n // 8, 8, TQ), axis=0))
        top = jnp.max(top, axis=0, keepdims=True)
        made = jnp.zeros((HEAD + 16, TQ), F32)
        for k, n in CHUNKS:
            p = jnp.exp2((scores[pl.ds(k, n), :] - top) * fold).astype(BF16)
            probs[t, pl.ds(k, n), :] = p
            made += jnp.dot(values_t[:, pl.ds(first + k, n)], p, preferred_element_type=F32)
        share = 1.0 / made[HEAD : HEAD + 1]
        shares[pl.ds(t, 1), :] = share
        out_t = made[:HEAD] * share
        outs_t[t] = out_t
        flows[pl.ds(first, TQ), :] = jnp.concatenate([out_t, out_t], axis=0).T.astype(BF16)

    @pl.loop(0, HEADS)
    def _(p):
        at = pl.multiple_of(p * points, 16)
        low, high = flows[pl.ds(at, side), :], flows[pl.ds(at + side, side), :]
        o_send[p] = jnp.concatenate([low[:, :HEAD], high[:, HEAD:]], axis=1)

    o_copies = [push(o_send.at[goals[i]], o_recv.at[place], o_ss.at[i], o_rs.at[i], mates[i]) for i in near]
    for copy in o_copies:
        copy.start()
    o_recv[place] = o_send[place]

    for copy in g_copies:
        copy.wait_recv()

    @pl.loop(0, HEADS)
    def _(p):
        a, b = q_recv[p], g_recv[p]
        at = pl.multiple_of(p * points, 16)
        qg[pl.ds(at, side), :] = jnp.concatenate([a[:, :HEAD], b[:, :HEAD]], axis=1)
        qg[pl.ds(at + side, side), :] = jnp.concatenate([a[:, HEAD:], b[:, HEAD:]], axis=1)

    def dq_copy(p):
        return push(dq_send.at[p], dq_recv.at[place], dq_ss.at[p], dq_rs.at[place], row * HEADS + p)

    def send_dq(p):
        at = pl.multiple_of(p * points, 16)
        low, high = flows[pl.ds(at, side), :], flows[pl.ds(at + side, side), :]
        dq_send[p] = jnp.concatenate([low[:, :HEAD], high[:, HEAD:]], axis=1)

        @pl.when(p != place)
        def _():
            dq_copy(p).start()

        @pl.when(p == place)
        def _():
            dq_recv[p] = dq_send[p]

    def back_copy(p):
        return push(kv_sum.at[block(p)], kv_back.at[place], b_ss.at[p], b_rs.at[place], row * HEADS + p)

    def send_back(p, rim, offset):
        value = acc[block(p, RIM), :]
        if rim is not None:
            value += rim_recv[rim, block(p, -offset), :].astype(F32)
        kv_sum[block(p), :] = value.astype(BF16)

        @pl.when(p != place)
        def _():
            back_copy(p).start()

        @pl.when(p == place)
        def _():
            kv_back[p] = kv_sum[block(p), :]

    rim_backs = [
        push(rim_send.at[0], rim_recv.at[1], back_ss.at[0], back_rs.at[0], lower),
        push(rim_send.at[1], rim_recv.at[0], back_ss.at[1], back_rs.at[1], upper),
    ]
    sib_copy = push(terms.at[1 - core], sib_recv, sib_ss, sib_rs, sibling)

    def to_sum(r):
        return pl.ds(pl.multiple_of(r * half, half), half)

    sum_ats = [to_sum(lax.rem(row + i, rows)) for i in range(rows)]
    s_copies = [push(half_sum.at[sum_ats[i + 1]], peer_recv.at[i], s_ss.at[i], s_rs.at[i], peers[i]) for i in far]
    place_in_half = place // 2
    z_goals = [core * (HEADS // 2) + j for j in range(HEADS // 2)]
    z_copies = [
        push(flat.at[pl.ds(j * part, part)], last_recv.at[place_in_half], z_ss.at[j], z_rs.at[place_in_half], row * HEADS + goal)
        for j, goal in enumerate(z_goals)
    ]

    low_lanes = lanes_low((TQ, 2 * HEAD))

    @pl.loop(0, span // TQ)
    def _(t):
        first = pl.multiple_of(t * TQ, TQ)
        query = qg[pl.ds(first, TQ), :]
        wide = query.astype(F32)
        slant = jnp.where(low_lanes, jnp.zeros_like(query), query)
        share = shares[pl.ds(t, 1), :]
        delta = jnp.sum(wide.T[HEAD:] * outs_t[t], axis=0, keepdims=True)
        scaled = wide * jnp.broadcast_to(share, (2 * HEAD, TQ)).T
        for_keys = jnp.where(low_lanes, scaled * scale, 0.0).astype(BF16)
        for_values = jnp.where(low_lanes, 0.0, scaled).astype(BF16)
        dq_t = jnp.zeros((HEAD, TQ), F32)
        for k, n in CHUNKS:
            turned = lax.dot_general(
                kv[pl.ds(first + k, n), :], slant, (((1,), (1,)), ((), ())), preferred_element_type=F32
            )
            p = probs[t, pl.ds(k, n), :]
            ds = p * (turned - delta).astype(BF16)
            dq_t += jnp.dot(keys_t[:, pl.ds(first + k, n)], ds, preferred_element_type=F32)
            acc[pl.ds(first + k, n), :] += jnp.dot(ds, for_keys, preferred_element_type=F32) + jnp.dot(
                p, for_values, preferred_element_type=F32
            )
        dq_t = dq_t * (share * scale)
        flows[pl.ds(first, TQ), :] = jnp.concatenate([dq_t, dq_t], axis=0).T.astype(BF16)

        @pl.when(t == 1)
        def _():
            for copy in o_copies:
                copy.wait_recv()
            split_up(o_recv, *halves(mixed))
            for k in range(HEADS // 2):
                term = lax.dot_general(
                    mixed[:, pl.ds(2 * HEAD * k, 2 * HEAD)], cot_ref[...], (((0,), (0,)), ((), ())),
                    preferred_element_type=F32,
                ).astype(BF16)
                for j in range(4):
                    terms[j % 2, pl.ds((2 * k + j // 2) * half, half), :] = term[j * half : (j + 1) * half]
            sib_copy.start()
            out_ref[...] = jnp.dot(mixed[...], weight[...], preferred_element_type=F32).astype(BF16)

        @pl.when(t == 2)
        def _():
            sib_copy.wait_recv()
            for i in range(rows):
                at = sum_ats[i]
                half_sum[at, :] = (terms[core, at, :].astype(F32) + sib_recv[at, :].astype(F32)).astype(BF16)
                if i:
                    s_copies[i - 1].start()

        @pl.when(t == 4)
        def _():
            rim_send[0] = acc[pl.ds(0, RIM), :].astype(BF16)
            rim_backs[0].start()
            for i in range(HEADS // 2):
                send_dq(lax.rem(place + i, HEADS // 2))

        @pl.when(t == 8)
        def _():
            total = half_sum[sum_ats[0], :].astype(F32)
            for i in far:
                s_copies[i].wait_recv()
                total += peer_recv[i].astype(F32)
            total = total * inverse_root
            for b in range(D // 128):
                flat[pl.ds(b, half, stride=D // 128), :] = total[:, b * 128 : (b + 1) * 128]
            for j, goal in enumerate(z_goals):

                @pl.when(goal != place)
                def _():
                    z_copies[j].start()

                @pl.when(goal == place)
                def _():
                    last_recv[place_in_half] = flat[pl.ds(j * part, part), :]

    rim_send[1] = acc[pl.ds(RIM + span, RIM), :].astype(BF16)
    rim_backs[1].start()
    rim_backs[0].wait_recv()
    free = RIM // points
    for i in range(HEADS - 2 * free):
        send_back(free + i, None, 0)
    for i in range(free):
        send_back(HEADS - free + lax.rem(place + i, free), 1, span - RIM)
    for i in range(HEADS // 2):
        send_dq(HEADS // 2 + lax.rem(place + i, HEADS // 2))
    rim_backs[1].wait_recv()
    for i in range(free):
        send_back(lax.rem(place + i, free), 0, 0)

    for z in range(HEADS // 2):
        source = 2 * z + place // (HEADS // 2)

        @pl.when(source != place)
        def _():
            push(flat.at[pl.ds(0, part)], last_recv.at[z], z_ss.at[0], z_rs.at[z], row * HEADS + source).wait_recv()

    dw_ref[...] = jnp.sum(last_recv[...], axis=0)

    for p in range(HEADS):

        @pl.when(p != place)
        def _():
            push(dq_send.at[p], dq_recv.at[p], dq_ss.at[p], dq_rs.at[p], row * HEADS + p).wait_recv()
            push(kv_sum.at[block(p)], kv_back.at[p], b_ss.at[p], b_rs.at[p], row * HEADS + p).wait_recv()
            dq_copy(p).wait_send()
            back_copy(p).wait_send()

    for goal, copy in zip(z_goals, z_copies, strict=True):

        @pl.when(goal != place)
        def _():
            copy.wait_send()

    for copies in (
        w_copies, kv_copies, st_copies, q_copies, x_copies, t_copies, rim_copies, g_copies, o_copies,
        rim_backs, [sib_copy], s_copies,
    ):
        for copy in copies:
            copy.wait_send()


def unpack_kernel(out_in, dq_in, kv_in, dw_in, out_ref, dq_ref, dk_ref, dv_ref, dw_ref):
    out_ref[...] = out_in[...]
    dw_ref[...] = dw_in[...]
    split_up(dq_in, *halves(dq_ref))
    split_up(kv_in, dk_ref, dv_ref)


def in_vmem(count):
    return [pl.BlockSpec(memory_space=pltpu.VMEM)] * count


def per_device(queries, key_rows, value_rows, out_weight, cotangent, row_lengths, window_shift):
    points = queries.shape[0]
    devices = lax.axis_size("seq")
    rows = devices // HEADS
    span = HEADS * points
    held = span + 2 * RIM
    tiles = span // TQ
    lanes = -(-held // 128) * 128
    w_part = out_weight.shape[0] // 128
    wide = 2 * HEAD
    half = HEAD // 2
    dma = pltpu.SemaphoreType.DMA
    ring, all_row, cross = dma((HEADS - 1,)), dma((HEADS,)), dma((rows - 1,))
    full = jax.ShapeDtypeStruct((points, D), BF16)
    sums = jax.ShapeDtypeStruct((w_part, 128), F32)
    blocks = pltpu.VMEM((HEADS, points, wide), BF16)
    packed = pltpu.VMEM((HEADS, points // 2, wide), BF16)
    made = pl.pallas_call(
        functools.partial(layer_kernel, rows, 1.0 / math.sqrt(devices * points)),
        out_shape=(
            full,
            jax.ShapeDtypeStruct((HEADS, points // 2, wide), BF16),
            jax.ShapeDtypeStruct((HEADS, points, wide), BF16),
            sums,
        ),
        in_specs=in_vmem(7),
        out_specs=tuple(in_vmem(4)),
        scratch_shapes=[
            blocks, packed, packed, packed, packed, packed, packed, packed,
            pltpu.VMEM((held, wide), BF16),
            pltpu.VMEM((span, wide), BF16),
            pltpu.VMEM((8, 256), jnp.int32),
            pltpu.VMEM((HEADS, 8, 256), jnp.int32),
            pltpu.VMEM((tiles, TQ), jnp.int32),
            pltpu.VMEM((HEADS * w_part, 128), BF16),
            pltpu.VMEM((HEADS * w_part, 128), F32),
            pltpu.VMEM((D, D), BF16),
            pltpu.VMEM((points, D), BF16),
            pltpu.VMEM((HEAD, lanes), BF16),
            pltpu.VMEM((HEAD + 16, lanes), BF16),
            pltpu.VMEM((held, wide), F32),
            pltpu.VMEM((SPAN, TQ), F32),
            pltpu.VMEM((tiles, SPAN, TQ), BF16),
            pltpu.VMEM((tiles, HEAD, TQ), F32),
            pltpu.VMEM((tiles, TQ), F32),
            pltpu.VMEM((span, wide), BF16),
            pltpu.VMEM((points, D), BF16),
            pltpu.VMEM((2, rows * half, D), BF16),
            pltpu.VMEM((rows * half, D), BF16),
            pltpu.VMEM((rows * half, D), BF16),
            pltpu.VMEM((rows - 1, half, D), BF16),
            pltpu.VMEM((half * D // 128, 128), F32),
            pltpu.VMEM((HEADS // 2, w_part, 128), F32),
            pltpu.VMEM((2, RIM, wide), BF16),
            pltpu.VMEM((2, RIM, wide), BF16),
            pltpu.VMEM((span, wide), BF16),
            ring, ring, ring, ring, ring, ring, ring, ring, ring, ring, ring, ring,
            all_row, all_row, all_row, all_row, cross, cross, cross, cross, cross, cross,
            dma((2,)), dma((2,)), dma((2,)), dma((2,)), dma, dma,
            dma((HEADS // 2,)), dma((HEADS // 2,)),
        ],
        compiler_params=pltpu.CompilerParams(
            collective_id=0, has_side_effects=True, vmem_limit_bytes=VMEM_LIMIT
        ),
        name="layer",
    )(
        queries, key_rows, value_rows, cotangent, out_weight.reshape(w_part, 128),
        row_lengths.reshape(1, -1), window_shift.reshape(1, -1),
    )
    out, dq, dk, dv, dw = pl.pallas_call(
        unpack_kernel,
        out_shape=(full, full, full, full, sums),
        in_specs=in_vmem(4),
        out_specs=tuple(in_vmem(5)),
        compiler_params=pltpu.CompilerParams(vmem_limit_bytes=VMEM_LIMIT),
        name="unpack",
    )(*made)
    return (out, dq, dk, dv, dw.reshape(-1))


def solution(mesh):
    whole = P("seq", None)
    return jax.shard_map(
        per_device,
        mesh=mesh,
        in_specs=(whole, whole, whole, P("seq"), whole, P(), P("seq")),
        out_specs=(whole, whole, whole, whole, P("seq")),
        check_vma=False,
    )
```

```python
import functools
import math

import jax
import jax.numpy as jnp
from jax import lax
from jax.experimental import pallas as pl
from jax.experimental.pallas import tpu as pltpu
from jax.sharding import PartitionSpec as P

D = 1024
HEADS = 16
HEAD = 64
WIN = 1120
RIM = 1120
TQ = 256
SPAN = 2496
CHUNKS = [(k, min(256, SPAN - k)) for k in range(0, SPAN, 256)]
LONG_CHUNKS = [(k, min(1280, SPAN - k)) for k in range(0, SPAN, 1280)]
FAR = -1e30
MESH = pl.DeviceIdType.MESH
BF16 = jnp.bfloat16
F32 = jnp.float32
VMEM_LIMIT = 56 * 1024 * 1024


def spot():
    me = lax.axis_index("seq")
    return me, me // HEADS, lax.rem(me, HEADS)


def push(src, dst, send, recv, device):
    return pltpu.make_async_remote_copy(
        src_ref=src, dst_ref=dst, send_sem=send, recv_sem=recv, device_id=(device,), device_id_type=MESH
    )


def lanes_low(shape):
    return lax.broadcasted_iota(jnp.int32, shape, 1) < HEAD


def pair_up(left, right, out):
    for k in range(HEADS // 2):
        cols = pl.ds(2 * HEAD * k, 2 * HEAD)
        a, b = left[:, cols], right[:, cols]
        out[2 * k] = jnp.concatenate([a[:, :HEAD], b[:, :HEAD]], axis=1)
        out[2 * k + 1] = jnp.concatenate([a[:, HEAD:], b[:, HEAD:]], axis=1)


def split_up(blocks, left, right):
    for k in range(HEADS // 2):
        cols = pl.ds(2 * HEAD * k, 2 * HEAD)
        a, b = blocks[2 * k], blocks[2 * k + 1]
        left[:, cols] = jnp.concatenate([a[:, :HEAD], b[:, :HEAD]], axis=1)
        right[:, cols] = jnp.concatenate([a[:, HEAD:], b[:, HEAD:]], axis=1)


def halves(ref):
    half = ref.shape[0] // 2
    return ref.at[pl.ds(0, half)], ref.at[pl.ds(half, half)]


def own_starts(len_ref, shift_ref, first_point, offset, all_points):
    count, points = len_ref.shape[1], shift_ref.shape[1]
    lens = jnp.concatenate([len_ref[...], jnp.zeros((1, 256 - count), jnp.int32)], axis=1)
    order = lax.broadcasted_iota(jnp.int32, (256, 256), 0)
    column = lax.broadcasted_iota(jnp.int32, (256, 256), 1)
    ends = jnp.sum(jnp.where(column <= order, lens, 0).astype(F32), axis=1, keepdims=True).astype(jnp.int32)
    lane = lax.broadcasted_iota(jnp.int32, (256, 256), 1)
    index = first_point + lane
    past = (ends <= index) & (order < count)
    row_first = jnp.max(jnp.where(past, jnp.broadcast_to(ends, (256, 256)), 0).astype(F32), axis=0, keepdims=True).astype(jnp.int32)
    shift = jnp.concatenate([shift_ref[...], jnp.zeros((1, 256 - points), jnp.int32)], axis=1)
    starts = jnp.clip(row_first - shift, 0, all_points - WIN)
    starts = jnp.where(lane[:1] < points, starts, 0)
    return pltpu.roll(jnp.broadcast_to(starts, (8, 256)), offset, 1)


def layer_kernel(
    rows, inverse_root,
    q_in, k_in, v_in, cot_in, w_ref, len_ref, shift_ref,
    out_ref, dq_recv, kv_back, dw_ref,
    q_ref, k_ref, v_ref, cot_ref,
    kq_send, v_send, v_recv, g_send, g_recv, o_send, o_recv, dq_send,
    v_rims, kq, vals, qg, st_send, st_recv, starts, w_recv, w_wide, weight, grad,
    keys_t, values_t, acc, scores, probs, outs_t, shares, flows,
    mixed, terms, sib_recv, half_sum, peer_recv, flat, last_recv,
    rim_send, rim_recv, kv_sum,
    in_sems,
    kv_ss, kv_rs, v_ss, v_rs, g_ss, g_rs, o_ss, o_rs, st_ss, st_rs, w_ss, w_rs,
    dq_ss, dq_rs, b_ss, b_rs, x_ss, x_rs, s_ss, s_rs, t_ss, t_rs, rim_ss, rim_rs, vr_ss, vr_rs, back_ss, back_rs, sib_ss, sib_rs,
    z_ss, z_rs,
):
    me, row, place = spot()
    core = lax.rem(me, 2)
    points = q_ref.shape[0]
    span = HEADS * points
    held = kq.shape[0]
    scale = 1.0 / math.sqrt(HEAD)
    fold = scale * math.log2(math.e)
    sibling = me + 1 - 2 * core
    near = range(HEADS - 1)
    far = range(rows - 1)
    goals = [lax.rem(place + i, HEADS) for i in range(1, HEADS)]
    mates = [row * HEADS + goal for goal in goals]
    peers = [lax.rem(row + i, rows) * HEADS + place for i in range(1, rows)]
    lower = lax.rem(row + rows - 1, rows) * HEADS + place
    upper = lax.rem(row + 1, rows) * HEADS + place

    def block(at, offset=0):
        return pl.ds(pl.multiple_of(offset + at * points, 16), points)

    barrier = pltpu.get_barrier_semaphore()
    for device in mates + peers:
        pl.semaphore_signal(barrier, inc=1, device_id=(device,), device_id_type=MESH)
    loads = [
        pltpu.make_async_copy(src, dst, in_sems.at[i])
        for i, (src, dst) in enumerate(((k_in, k_ref), (q_in, q_ref), (v_in, v_ref), (cot_in, cot_ref)))
    ]
    for copy in loads:
        copy.start()
    loads[0].wait()
    loads[1].wait()
    pair_up(k_ref, q_ref, kq_send)
    pl.semaphore_wait(barrier, len(mates) + len(peers))

    part = w_ref.shape[0]
    w_at = pl.ds(pl.multiple_of(place * part, part), part)
    w_copies = [push(w_ref, w_recv.at[w_at], w_ss.at[i], w_rs.at[i], mates[i]) for i in near]
    kv_copies = [push(kq_send.at[goals[i]], kq.at[block(place, RIM)], kv_ss.at[i], kv_rs.at[i], mates[i]) for i in near]
    v_copies = [push(v_send.at[goals[i]], v_recv.at[place], v_ss.at[i], v_rs.at[i], mates[i]) for i in near]
    st_copies = [push(st_send, st_recv.at[place], st_ss.at[i], st_rs.at[i], mates[i]) for i in near]
    for copy in w_copies + kv_copies:
        copy.start()
    loads[2].wait()
    pair_up(*halves(v_ref), v_send)
    for copy in v_copies:
        copy.start()
    st_send[...] = own_starts(
        len_ref, shift_ref, me * points, lax.rem(place * points, 128), rows * span
    )
    for copy in st_copies:
        copy.start()
    w_recv[w_at] = w_ref[...]
    kq[block(place, RIM), :] = kq_send[place]
    v_recv[place] = v_send[place]
    st_recv[place] = st_send[...]

    for copy in w_copies:
        copy.wait_recv()
    w_wide[...] = w_recv[...].astype(F32)
    wrows = HEADS * part * 2 * HEAD // D
    half = wrows // 2
    own = pl.multiple_of(row * wrows, 16)
    for b in range(D // 128):
        weight[pl.ds(own, wrows), pl.ds(b * 128, 128)] = w_wide[pl.ds(b, wrows, stride=D // 128), :].astype(BF16)
    my_half = weight.at[pl.ds(pl.multiple_of(own + core * half, 16), half)]
    x_copies = [push(my_half, my_half, x_ss.at[i], x_rs.at[i], peers[i]) for i in far]
    for copy in x_copies:
        copy.start()

    @pl.loop(0, held // 160)
    def _(t):
        acc[pl.ds(pl.multiple_of(t * 160, 160), 160), :] = jnp.zeros((160, 2 * HEAD), F32)

    values_t[HEAD:, :] = jnp.ones((16, values_t.shape[1]), BF16)

    rim_blocks = RIM // points

    def rim_down(p):
        return push(kq.at[block(p, RIM)], kq.at[block(p, RIM + span)], rim_ss.at[p], rim_rs.at[p], lower)

    def rim_up(p):
        at = p - (HEADS - rim_blocks)
        return push(kq.at[block(p, RIM)], kq.at[block(at)], rim_ss.at[p], rim_rs.at[p], upper)

    def rim_on(p):
        @pl.when(p < rim_blocks)
        def _():
            rim_down(p).start()

        @pl.when(p >= HEADS - rim_blocks)
        def _():
            rim_up(p).start()

    rim_on(place)
    for i in near:
        kv_copies[i].wait_recv()
        rim_on(lax.rem(place + HEADS - i - 1, HEADS))
    rim_copies = [rim_down(p) for p in range(rim_blocks)] + [rim_up(p) for p in range(HEADS - rim_blocks, HEADS)]

    side = points // 2

    def v_down(p):
        return push(v_recv.at[p], v_rims.at[p + rim_blocks], vr_ss.at[p], vr_rs.at[p], lower)

    def v_up(p):
        return push(v_recv.at[p], v_rims.at[p - (HEADS - rim_blocks)], vr_ss.at[p], vr_rs.at[p], upper)

    def v_on(p):
        @pl.when(p < rim_blocks)
        def _():
            v_down(p).start()

        @pl.when(p >= HEADS - rim_blocks)
        def _():
            v_up(p).start()

    v_rim_copies = [v_down(p) for p in range(rim_blocks)] + [v_up(p) for p in range(HEADS - rim_blocks, HEADS)]

    def lay_values(packed, at):
        vals[pl.ds(at, side), :] = packed[:, :HEAD]
        vals[pl.ds(at + side, side), :] = packed[:, HEAD:]

    def turn(at, size):
        keys_t[:, pl.ds(at, size)] = kq[pl.ds(at, size), :].astype(F32).T[:HEAD].astype(BF16)
        values_t[:HEAD, pl.ds(at, size)] = vals[pl.ds(at, size), :].astype(F32).T.astype(BF16)

    sources = [lax.rem(row + rows - i - 1, rows) for i in far]
    came = [weight.at[pl.ds(pl.multiple_of(r * wrows + core * half, 16), half)] for r in sources]
    t_copies = [push(came[i], came[i], t_ss.at[i], t_rs.at[i], sibling) for i in far]
    g_copies = [push(g_send.at[goals[i]], g_recv.at[place], g_ss.at[i], g_rs.at[i], mates[i]) for i in near]

    for copy in st_copies:
        copy.wait_recv()
    for t in range(span // 128):
        total = None
        for p in range(HEADS):
            first = p * points // 128
            if first <= t <= first + 1:
                piece = st_recv[p, 0:1, pl.ds((t - first) * 128, 128)]
                total = piece if total is None else total + piece
        starts[t // 2 : t // 2 + 1, (t % 2) * 128 : (t % 2 + 1) * 128] = total
    for copy in rim_copies:
        copy.wait_recv()

    base = row * span - RIM
    tiles = span // TQ
    half_row = HEADS // 2

    def o_copy(p):
        return push(o_send.at[p], o_recv.at[place], o_ss.at[p], o_rs.at[place], row * HEADS + p)

    def send_o(p):
        at = pl.multiple_of(p * points, 16)
        low, high = flows[pl.ds(at, side), :], flows[pl.ds(at + side, side), :]
        o_send[p] = jnp.concatenate([low[:, :HEAD], high[:, HEAD:]], axis=1)

        @pl.when(p != place)
        def _():
            o_copy(p).start()

        @pl.when(p == place)
        def _():
            o_recv[p] = o_send[p]

    @pl.loop(0, span // TQ)
    def _(t):
        first = pl.multiple_of(t * TQ, TQ)
        query = kq[pl.ds(pl.multiple_of(first + RIM, 16), TQ), HEAD:]
        query = jnp.concatenate([query, jnp.zeros_like(query)], axis=1)
        rel = starts[pl.ds(t, 1), :] - base - first
        top = jnp.full((8, TQ), FAR, F32)
        for k, n in CHUNKS:
            s = lax.dot_general(
                kq[pl.ds(first + k, n), :], query, (((1,), (1,)), ((), ())), preferred_element_type=F32
            )
            past = lax.broadcasted_iota(jnp.int32, (n, TQ), 0) - (rel - k)
            s = jnp.where(past.astype(jnp.uint32) < jnp.uint32(WIN), s, FAR)
            scores[pl.ds(k, n), :] = s
            top = jnp.maximum(top, jnp.max(s.reshape(n // 8, 8, TQ), axis=0))
        top = jnp.max(top, axis=0, keepdims=True)
        for k, n in CHUNKS:
            probs[t, pl.ds(k, n), :] = jnp.exp2((scores[pl.ds(k, n), :] - top) * fold).astype(BF16)

        @pl.when(t == 1)
        def _():
            for i in far:
                x_copies[i].wait_recv()
                t_copies[i].start()

        @pl.when(t == 4)
        def _():
            for copy in t_copies:
                copy.wait_recv()
            loads[3].wait()
            grad[...] = lax.dot_general(
                cot_ref[...], weight[...], (((1,), (1,)), ((), ())), preferred_element_type=F32
            ).astype(BF16)
            pair_up(*halves(grad), g_send)
            for copy in g_copies:
                copy.start()
            g_recv[place] = g_send[place]

        @pl.when(t == 3)
        def _():
            v_on(place)
            for i in near:
                v_copies[i].wait_recv()
                v_on(lax.rem(place + HEADS - i - 1, HEADS))

    @pl.loop(0, HEADS)
    def _(p):
        lay_values(v_recv[p], pl.multiple_of(RIM + p * points, 16))

    for copy in v_rim_copies:
        copy.wait_recv()

    @pl.loop(0, rim_blocks)
    def _(p):
        lay_values(v_rims[p], pl.multiple_of(p * points, 16))
        lay_values(v_rims[p + rim_blocks], pl.multiple_of(RIM + span + p * points, 16))

    @pl.loop(0, held // 128)
    def _(t):
        turn(pl.multiple_of(t * 128, 128), 128)

    turn(held // 128 * 128, held % 128)

    @pl.loop(0, span // TQ)
    def _(step):
        t = lax.rem(step + core * (tiles // 2), tiles)
        first = pl.multiple_of(t * TQ, TQ)
        made = jnp.dot(values_t[:, pl.ds(first, SPAN)], probs[t], preferred_element_type=F32)
        share = 1.0 / made[HEAD : HEAD + 1]
        shares[pl.ds(t, 1), :] = share
        out_t = made[:HEAD] * share
        outs_t[t] = out_t
        flows[pl.ds(first, TQ), :] = jnp.concatenate([out_t, out_t], axis=0).T.astype(BF16)

        @pl.when(step == tiles // 2 - 1)
        def _():
            for i in range(half_row):
                send_o(core * half_row + lax.rem(place + i, half_row))

    for i in range(half_row):
        send_o((1 - core) * half_row + lax.rem(place + i, half_row))

    for copy in g_copies:
        copy.wait_recv()

    @pl.loop(0, HEADS)
    def _(p):
        b = g_recv[p]
        at = pl.multiple_of(p * points, 16)
        low = kq[pl.ds(pl.multiple_of(at + RIM, 16), side), HEAD:]
        high = kq[pl.ds(pl.multiple_of(at + side + RIM, 16), side), HEAD:]
        qg[pl.ds(at, side), :] = jnp.concatenate([low, b[:, :HEAD]], axis=1)
        qg[pl.ds(at + side, side), :] = jnp.concatenate([high, b[:, HEAD:]], axis=1)

    def dq_copy(p):
        return push(dq_send.at[p], dq_recv.at[place], dq_ss.at[p], dq_rs.at[place], row * HEADS + p)

    def send_dq(p):
        at = pl.multiple_of(p * points, 16)
        low, high = flows[pl.ds(at, side), :], flows[pl.ds(at + side, side), :]
        dq_send[p] = jnp.concatenate([low[:, :HEAD], high[:, HEAD:]], axis=1)

        @pl.when(p != place)
        def _():
            dq_copy(p).start()

        @pl.when(p == place)
        def _():
            dq_recv[p] = dq_send[p]

    def back_copy(p):
        return push(kv_sum.at[block(p)], kv_back.at[place], b_ss.at[p], b_rs.at[place], row * HEADS + p)

    def send_back(p, rim, at):
        value = acc[block(p, RIM), :]
        if rim is not None:
            value += rim_recv[rim, block(at), :].astype(F32)
        kv_sum[block(p), :] = value.astype(BF16)

        @pl.when(p != place)
        def _():
            back_copy(p).start()

        @pl.when(p == place)
        def _():
            kv_back[p] = kv_sum[block(p), :]

    towards = lower + core * (upper - lower)
    rim_backs = [
        push(rim_send.at[0], rim_recv.at[1 - core], back_ss.at[0], back_rs.at[0], towards),
        push(rim_send.at[1], rim_recv.at[core], back_ss.at[1], back_rs.at[1], lower + upper - towards),
    ]

    def send_rim(i, side_of_row):
        at = pl.multiple_of(side_of_row * (RIM + span), 16)
        rim_send[i] = acc[pl.ds(at, RIM), :].astype(BF16)
        rim_backs[i].start()

    sib_copy = push(terms.at[1 - core], sib_recv, sib_ss, sib_rs, sibling)

    def to_sum(r):
        return pl.ds(pl.multiple_of(r * half, half), half)

    sum_ats = [to_sum(lax.rem(row + i, rows)) for i in range(rows)]
    s_copies = [push(half_sum.at[sum_ats[i + 1]], peer_recv.at[i], s_ss.at[i], s_rs.at[i], peers[i]) for i in far]
    place_in_half = place // 2
    z_goals = [core * (HEADS // 2) + j for j in range(HEADS // 2)]
    z_copies = [
        push(flat.at[pl.ds(j * part, part)], last_recv.at[place_in_half], z_ss.at[j], z_rs.at[place_in_half], row * HEADS + goal)
        for j, goal in enumerate(z_goals)
    ]

    low_lanes = lanes_low((TQ, 2 * HEAD))

    @pl.loop(0, span // TQ)
    def _(step):
        t = lax.rem(step + core * (tiles // 2), tiles)
        first = pl.multiple_of(t * TQ, TQ)
        query = qg[pl.ds(first, TQ), :]
        wide = query.astype(F32)
        slant = query[:, HEAD:]
        share = shares[pl.ds(t, 1), :]
        delta = jnp.sum(wide.T[HEAD:] * outs_t[t], axis=0, keepdims=True)
        scaled = wide * jnp.broadcast_to(share, (2 * HEAD, TQ)).T
        for_keys = jnp.where(low_lanes, scaled * scale, 0.0).astype(BF16)
        for_values = jnp.where(low_lanes, 0.0, scaled).astype(BF16)
        dq_t = jnp.zeros((HEAD, TQ), F32)
        for k, n in LONG_CHUNKS:
            turned = lax.dot_general(
                vals[pl.ds(first + k, n), :], slant, (((1,), (1,)), ((), ())), preferred_element_type=F32
            )
            p = probs[t, pl.ds(k, n), :]
            ds = p * (turned - delta).astype(BF16)
            dq_t += jnp.dot(keys_t[:, pl.ds(first + k, n)], ds, preferred_element_type=F32)
            acc[pl.ds(first + k, n), :] += jnp.dot(ds, for_keys, preferred_element_type=F32) + jnp.dot(
                p, for_values, preferred_element_type=F32
            )
        dq_t = dq_t * (share * scale)
        flows[pl.ds(first, TQ), :] = jnp.concatenate([dq_t, dq_t], axis=0).T.astype(BF16)

        @pl.when(step == 5)
        def _():
            for p in range(HEADS):

                @pl.when(p != place)
                def _():
                    push(o_send.at[p], o_recv.at[p], o_ss.at[p], o_rs.at[p], row * HEADS + p).wait_recv()

            split_up(o_recv, *halves(mixed))
            for k in range(HEADS // 2):
                term = lax.dot_general(
                    mixed[:, pl.ds(2 * HEAD * k, 2 * HEAD)], cot_ref[...], (((0,), (0,)), ((), ())),
                    preferred_element_type=F32,
                ).astype(BF16)
                for j in range(4):
                    terms[j % 2, pl.ds((2 * k + j // 2) * half, half), :] = term[j * half : (j + 1) * half]
            sib_copy.start()
            out_ref[...] = jnp.dot(mixed[...], weight[...], preferred_element_type=F32).astype(BF16)

        @pl.when(step == 8)
        def _():
            sib_copy.wait_recv()
            for i in range(rows):
                at = sum_ats[i]
                half_sum[at, :] = (terms[core, at, :].astype(F32) + sib_recv[at, :].astype(F32)).astype(BF16)

        @pl.when(step == 4)
        def _():
            send_rim(0, core)
            for i in range(half_row):
                send_dq(core * half_row + lax.rem(place + i, half_row))

    send_rim(1, 1 - core)
    for copy in s_copies:
        copy.start()
    for i in range(half_row):
        send_dq((1 - core) * half_row + lax.rem(place + i, half_row))
    free = rim_blocks
    for i in range(HEADS - 2 * free):
        send_back(free + i, None, None)
    rim_backs[0].wait_recv()
    for i in range(free):
        at = lax.rem(place + i, free)
        send_back((1 - core) * (HEADS - free) + at, 1 - core, at)
    rim_backs[1].wait_recv()
    for i in range(free):
        at = lax.rem(place + i, free)
        send_back(core * (HEADS - free) + at, core, at)

    total = half_sum[sum_ats[0], :].astype(F32)
    for i in far:
        s_copies[i].wait_recv()
        total += peer_recv[i].astype(F32)
    total = total * inverse_root
    for b in range(D // 128):
        flat[pl.ds(b, half, stride=D // 128), :] = total[:, b * 128 : (b + 1) * 128]
    for j, goal in enumerate(z_goals):

        @pl.when(goal != place)
        def _():
            z_copies[j].start()

        @pl.when(goal == place)
        def _():
            last_recv[place_in_half] = flat[pl.ds(j * part, part), :]

    for z in range(HEADS // 2):
        source = 2 * z + place // (HEADS // 2)

        @pl.when(source != place)
        def _():
            push(flat.at[pl.ds(0, part)], last_recv.at[z], z_ss.at[0], z_rs.at[z], row * HEADS + source).wait_recv()

    dw_ref[...] = jnp.sum(last_recv[...], axis=0)

    for p in range(HEADS):

        @pl.when(p != place)
        def _():
            push(dq_send.at[p], dq_recv.at[p], dq_ss.at[p], dq_rs.at[p], row * HEADS + p).wait_recv()
            push(kv_sum.at[block(p)], kv_back.at[p], b_ss.at[p], b_rs.at[p], row * HEADS + p).wait_recv()
            dq_copy(p).wait_send()
            o_copy(p).wait_send()
            back_copy(p).wait_send()

    for goal, copy in zip(z_goals, z_copies, strict=True):

        @pl.when(goal != place)
        def _():
            copy.wait_send()

    for copies in (
        w_copies, kv_copies, st_copies, v_copies, x_copies, t_copies, rim_copies, v_rim_copies, g_copies,
        rim_backs, [sib_copy], s_copies,
    ):
        for copy in copies:
            copy.wait_send()


def unpack_kernel(out_in, dq_in, kv_in, dw_in, out_ref, dq_ref, dk_ref, dv_ref, dw_ref):
    out_ref[...] = out_in[...]
    dw_ref[...] = dw_in[...]
    split_up(dq_in, *halves(dq_ref))
    split_up(kv_in, dk_ref, dv_ref)


def in_vmem(count):
    return [pl.BlockSpec(memory_space=pltpu.VMEM)] * count


def anywhere(count):
    return [pl.BlockSpec(memory_space=pl.ANY)] * count


def per_device(queries, key_rows, value_rows, out_weight, cotangent, row_lengths, window_shift):
    points = queries.shape[0]
    devices = lax.axis_size("seq")
    rows = devices // HEADS
    span = HEADS * points
    held = span + 2 * RIM
    tiles = span // TQ
    lanes = -(-held // 128) * 128
    w_part = out_weight.shape[0] // 128
    wide = 2 * HEAD
    half = HEAD // 2
    dma = pltpu.SemaphoreType.DMA
    ring, all_row, cross = dma((HEADS - 1,)), dma((HEADS,)), dma((rows - 1,))
    full = jax.ShapeDtypeStruct((points, D), BF16)
    own = pltpu.VMEM((points, D), BF16)
    sums = jax.ShapeDtypeStruct((w_part, 128), F32)
    blocks = pltpu.VMEM((HEADS, points, wide), BF16)
    packed = pltpu.VMEM((HEADS, points // 2, wide), BF16)
    made = pl.pallas_call(
        functools.partial(layer_kernel, rows, 1.0 / math.sqrt(devices * points)),
        out_shape=(
            full,
            jax.ShapeDtypeStruct((HEADS, points // 2, wide), BF16),
            jax.ShapeDtypeStruct((HEADS, points, wide), BF16),
            sums,
        ),
        in_specs=anywhere(4) + in_vmem(3),
        out_specs=tuple(in_vmem(4)),
        scratch_shapes=[
            own, own, own, own,
            blocks, packed, packed, packed, packed, packed, packed, packed,
            pltpu.VMEM((2 * RIM // points, points // 2, wide), BF16),
            pltpu.VMEM((held, wide), BF16),
            pltpu.VMEM((held, HEAD), BF16),
            pltpu.VMEM((span, wide), BF16),
            pltpu.VMEM((8, 256), jnp.int32),
            pltpu.VMEM((HEADS, 8, 256), jnp.int32),
            pltpu.VMEM((tiles, TQ), jnp.int32),
            pltpu.VMEM((HEADS * w_part, 128), BF16),
            pltpu.VMEM((HEADS * w_part, 128), F32),
            pltpu.VMEM((D, D), BF16),
            pltpu.VMEM((points, D), BF16),
            pltpu.VMEM((HEAD, lanes), BF16),
            pltpu.VMEM((HEAD + 16, lanes), BF16),
            pltpu.VMEM((held, wide), F32),
            pltpu.VMEM((SPAN, TQ), F32),
            pltpu.VMEM((tiles, SPAN, TQ), BF16),
            pltpu.VMEM((tiles, HEAD, TQ), F32),
            pltpu.VMEM((tiles, TQ), F32),
            pltpu.VMEM((span, wide), BF16),
            pltpu.VMEM((points, D), BF16),
            pltpu.VMEM((2, rows * half, D), BF16),
            pltpu.VMEM((rows * half, D), BF16),
            pltpu.VMEM((rows * half, D), BF16),
            pltpu.VMEM((rows - 1, half, D), BF16),
            pltpu.VMEM((half * D // 128, 128), F32),
            pltpu.VMEM((HEADS // 2, w_part, 128), F32),
            pltpu.VMEM((2, RIM, wide), BF16),
            pltpu.VMEM((2, RIM, wide), BF16),
            pltpu.VMEM((span, wide), BF16),
            dma((4,)),
            ring, ring, ring, ring, ring, ring, all_row, all_row, ring, ring, ring, ring,
            all_row, all_row, all_row, all_row, cross, cross, cross, cross, cross, cross,
            all_row, all_row, all_row, all_row, dma((2,)), dma((2,)), dma, dma,
            dma((HEADS // 2,)), dma((HEADS // 2,)),
        ],
        compiler_params=pltpu.CompilerParams(
            collective_id=0, has_side_effects=True, vmem_limit_bytes=VMEM_LIMIT
        ),
        name="layer",
    )(
        queries, key_rows, value_rows, cotangent, out_weight.reshape(w_part, 128),
        row_lengths.reshape(1, -1), window_shift.reshape(1, -1),
    )
    out, dq, dk, dv, dw = pl.pallas_call(
        unpack_kernel,
        out_shape=(full, full, full, full, sums),
        in_specs=in_vmem(4),
        out_specs=tuple(in_vmem(5)),
        compiler_params=pltpu.CompilerParams(vmem_limit_bytes=VMEM_LIMIT),
        name="unpack",
    )(*made)
    return (out, dq, dk, dv, dw.reshape(-1))


def solution(mesh):
    whole = P("seq", None)
    return jax.shard_map(
        per_device,
        mesh=mesh,
        in_specs=(whole, whole, whole, P("seq"), whole, P(), P("seq")),
        out_specs=(whole, whole, whole, whole, P("seq")),
        check_vma=False,
    )
```

```python
import functools
import math

import jax
import jax.numpy as jnp
from jax import lax
from jax.experimental import pallas as pl
from jax.experimental.pallas import tpu as pltpu
from jax.sharding import PartitionSpec as P

D = 1024
HEADS = 16
HEAD = 64
WIN = 1120
RIM = 1120
TQ = 256
SPAN = 2496
CHUNKS = [(k, min(256, SPAN - k)) for k in range(0, SPAN, 256)]
LONG_CHUNKS = [(k, min(1280, SPAN - k)) for k in range(0, SPAN, 1280)]
FAR = -1e30
MESH = pl.DeviceIdType.MESH
BF16 = jnp.bfloat16
F32 = jnp.float32
VMEM_LIMIT = 56 * 1024 * 1024


def spot():
    me = lax.axis_index("seq")
    return me, me // HEADS, lax.rem(me, HEADS)


def push(src, dst, send, recv, device):
    return pltpu.make_async_remote_copy(
        src_ref=src, dst_ref=dst, send_sem=send, recv_sem=recv, device_id=(device,), device_id_type=MESH
    )


def lanes_low(shape):
    return lax.broadcasted_iota(jnp.int32, shape, 1) < HEAD


def pair_up(left, right, out):
    for k in range(HEADS // 2):
        cols = pl.ds(2 * HEAD * k, 2 * HEAD)
        a, b = left[:, cols], right[:, cols]
        out[2 * k] = jnp.concatenate([a[:, :HEAD], b[:, :HEAD]], axis=1)
        out[2 * k + 1] = jnp.concatenate([a[:, HEAD:], b[:, HEAD:]], axis=1)


def split_up(blocks, left, right):
    for k in range(HEADS // 2):
        cols = pl.ds(2 * HEAD * k, 2 * HEAD)
        a, b = blocks[2 * k], blocks[2 * k + 1]
        left[:, cols] = jnp.concatenate([a[:, :HEAD], b[:, :HEAD]], axis=1)
        right[:, cols] = jnp.concatenate([a[:, HEAD:], b[:, HEAD:]], axis=1)


def halves(ref):
    half = ref.shape[0] // 2
    return ref.at[pl.ds(0, half)], ref.at[pl.ds(half, half)]


def own_starts(len_ref, shift_ref, first_point, offset, all_points):
    count, points = len_ref.shape[1], shift_ref.shape[1]
    lens = jnp.concatenate([len_ref[...], jnp.zeros((1, 256 - count), jnp.int32)], axis=1)
    order = lax.broadcasted_iota(jnp.int32, (256, 256), 0)
    column = lax.broadcasted_iota(jnp.int32, (256, 256), 1)
    ends = jnp.sum(jnp.where(column <= order, lens, 0).astype(F32), axis=1, keepdims=True).astype(jnp.int32)
    lane = lax.broadcasted_iota(jnp.int32, (256, 256), 1)
    index = first_point + lane
    past = (ends <= index) & (order < count)
    row_first = jnp.max(jnp.where(past, jnp.broadcast_to(ends, (256, 256)), 0).astype(F32), axis=0, keepdims=True).astype(jnp.int32)
    shift = jnp.concatenate([shift_ref[...], jnp.zeros((1, 256 - points), jnp.int32)], axis=1)
    starts = jnp.clip(row_first - shift, 0, all_points - WIN)
    starts = jnp.where(lane[:1] < points, starts, 0)
    return pltpu.roll(jnp.broadcast_to(starts, (8, 256)), offset, 1)


def layer_kernel(
    rows, inverse_root,
    q_in, k_in, v_in, cot_in, w_ref, len_ref, shift_ref,
    out_ref, dq_recv, kv_back, dw_ref,
    q_ref, k_ref, v_ref, cot_ref,
    kq_send, v_send, v_recv, g_send, g_recv, o_send, o_recv, dq_send,
    v_rims, kq, vals, qg, st_send, st_recv, starts, w_recv, w_wide, weight, grad,
    keys_t, values_t, acc, scores, probs, outs_t, shares, flows,
    mixed, terms, sib_recv, half_sum, peer_recv, flat, last_recv,
    rim_send, rim_recv, kv_sum,
    in_sems,
    kv_ss, kv_rs, v_ss, v_rs, g_ss, g_rs, o_ss, o_rs, st_ss, st_rs, w_ss, w_rs,
    dq_ss, dq_rs, b_ss, b_rs, x_ss, x_rs, s_ss, s_rs, t_ss, t_rs, rim_ss, rim_rs, vr_ss, vr_rs, back_ss, back_rs, sib_ss, sib_rs,
    z_ss, z_rs,
):
    me, row, place = spot()
    core = lax.rem(me, 2)
    back = lax.rem(core + row, 2)
    points = q_ref.shape[0]
    span = HEADS * points
    held = kq.shape[0]
    scale = 1.0 / math.sqrt(HEAD)
    fold = scale * math.log2(math.e)
    sibling = me + 1 - 2 * core
    near = range(HEADS - 1)
    far = range(rows - 1)
    goals = [lax.rem(place + i, HEADS) for i in range(1, HEADS)]
    mates = [row * HEADS + goal for goal in goals]
    peers = [lax.rem(row + i, rows) * HEADS + place for i in range(1, rows)]
    lower = lax.rem(row + rows - 1, rows) * HEADS + place
    upper = lax.rem(row + 1, rows) * HEADS + place

    def block(at, offset=0):
        return pl.ds(pl.multiple_of(offset + at * points, 16), points)

    barrier = pltpu.get_barrier_semaphore()
    for device in mates + peers:
        pl.semaphore_signal(barrier, inc=1, device_id=(device,), device_id_type=MESH)
    loads = [
        pltpu.make_async_copy(src, dst, in_sems.at[i])
        for i, (src, dst) in enumerate(((k_in, k_ref), (q_in, q_ref), (v_in, v_ref), (cot_in, cot_ref)))
    ]
    for copy in loads:
        copy.start()
    loads[0].wait()
    loads[1].wait()
    pair_up(k_ref, q_ref, kq_send)
    pl.semaphore_wait(barrier, len(mates) + len(peers))

    part = w_ref.shape[0]
    w_at = pl.ds(pl.multiple_of(place * part, part), part)
    w_copies = [push(w_ref, w_recv.at[w_at], w_ss.at[i], w_rs.at[i], mates[i]) for i in near]
    kv_copies = [push(kq_send.at[goals[i]], kq.at[block(place, RIM)], kv_ss.at[i], kv_rs.at[i], mates[i]) for i in near]
    v_copies = [push(v_send.at[goals[i]], v_recv.at[place], v_ss.at[i], v_rs.at[i], mates[i]) for i in near]
    st_copies = [push(st_send, st_recv.at[place], st_ss.at[i], st_rs.at[i], mates[i]) for i in near]
    for copy in w_copies + kv_copies:
        copy.start()
    loads[2].wait()
    pair_up(*halves(v_ref), v_send)
    for copy in v_copies:
        copy.start()
    st_send[...] = own_starts(
        len_ref, shift_ref, me * points, lax.rem(place * points, 128), rows * span
    )
    for copy in st_copies:
        copy.start()
    w_recv[w_at] = w_ref[...]
    kq[block(place, RIM), :] = kq_send[place]
    v_recv[place] = v_send[place]
    st_recv[place] = st_send[...]

    for copy in w_copies:
        copy.wait_recv()
    w_wide[...] = w_recv[...].astype(F32)
    wrows = HEADS * part * 2 * HEAD // D
    half = wrows // 2
    own = pl.multiple_of(row * wrows, 16)
    for b in range(D // 128):
        weight[pl.ds(own, wrows), pl.ds(b * 128, 128)] = w_wide[pl.ds(b, wrows, stride=D // 128), :].astype(BF16)
    my_half = weight.at[pl.ds(pl.multiple_of(own + core * half, 16), half)]
    x_copies = [push(my_half, my_half, x_ss.at[i], x_rs.at[i], peers[i]) for i in far]
    for copy in x_copies:
        copy.start()

    @pl.loop(0, held // 160)
    def _(t):
        acc[pl.ds(pl.multiple_of(t * 160, 160), 160), :] = jnp.zeros((160, 2 * HEAD), F32)

    values_t[HEAD:, :] = jnp.ones((16, values_t.shape[1]), BF16)

    rim_blocks = RIM // points

    def rim_down(p):
        return push(kq.at[block(p, RIM)], kq.at[block(p, RIM + span)], rim_ss.at[p], rim_rs.at[p], lower)

    def rim_up(p):
        at = p - (HEADS - rim_blocks)
        return push(kq.at[block(p, RIM)], kq.at[block(at)], rim_ss.at[p], rim_rs.at[p], upper)

    def rim_on(p):
        @pl.when(p < rim_blocks)
        def _():
            rim_down(p).start()

        @pl.when(p >= HEADS - rim_blocks)
        def _():
            rim_up(p).start()

    rim_on(place)
    for i in near:
        kv_copies[i].wait_recv()
        rim_on(lax.rem(place + HEADS - i - 1, HEADS))
    rim_copies = [rim_down(p) for p in range(rim_blocks)] + [rim_up(p) for p in range(HEADS - rim_blocks, HEADS)]

    side = points // 2

    def v_down(p):
        return push(v_recv.at[p], v_rims.at[p + rim_blocks], vr_ss.at[p], vr_rs.at[p], lower)

    def v_up(p):
        return push(v_recv.at[p], v_rims.at[p - (HEADS - rim_blocks)], vr_ss.at[p], vr_rs.at[p], upper)

    def v_on(p):
        @pl.when(p < rim_blocks)
        def _():
            v_down(p).start()

        @pl.when(p >= HEADS - rim_blocks)
        def _():
            v_up(p).start()

    v_rim_copies = [v_down(p) for p in range(rim_blocks)] + [v_up(p) for p in range(HEADS - rim_blocks, HEADS)]

    def lay_values(packed, at):
        vals[pl.ds(at, side), :] = packed[:, :HEAD]
        vals[pl.ds(at + side, side), :] = packed[:, HEAD:]

    def turn(at, size):
        keys_t[:, pl.ds(at, size)] = kq[pl.ds(at, size), :].astype(F32).T[:HEAD].astype(BF16)
        values_t[:HEAD, pl.ds(at, size)] = vals[pl.ds(at, size), :].astype(F32).T.astype(BF16)

    sources = [lax.rem(row + rows - i - 1, rows) for i in far]
    came = [weight.at[pl.ds(pl.multiple_of(r * wrows + core * half, 16), half)] for r in sources]
    t_copies = [push(came[i], came[i], t_ss.at[i], t_rs.at[i], sibling) for i in far]
    g_copies = [push(g_send.at[goals[i]], g_recv.at[place], g_ss.at[i], g_rs.at[i], mates[i]) for i in near]

    for copy in st_copies:
        copy.wait_recv()
    for t in range(span // 128):
        total = None
        for p in range(HEADS):
            first = p * points // 128
            if first <= t <= first + 1:
                piece = st_recv[p, 0:1, pl.ds((t - first) * 128, 128)]
                total = piece if total is None else total + piece
        starts[t // 2 : t // 2 + 1, (t % 2) * 128 : (t % 2 + 1) * 128] = total
    for copy in rim_copies:
        copy.wait_recv()

    base = row * span - RIM
    tiles = span // TQ
    half_row = HEADS // 2

    def o_copy(p):
        return push(o_send.at[p], o_recv.at[place], o_ss.at[p], o_rs.at[place], row * HEADS + p)

    def send_o(p):
        at = pl.multiple_of(p * points, 16)
        low, high = flows[pl.ds(at, side), :], flows[pl.ds(at + side, side), :]
        o_send[p] = jnp.concatenate([low[:, :HEAD], high[:, HEAD:]], axis=1)

        @pl.when(p != place)
        def _():
            o_copy(p).start()

        @pl.when(p == place)
        def _():
            o_recv[p] = o_send[p]

    @pl.loop(0, span // TQ)
    def _(t):
        first = pl.multiple_of(t * TQ, TQ)
        query = kq[pl.ds(pl.multiple_of(first + RIM, 16), TQ), HEAD:]
        query = jnp.concatenate([query, jnp.zeros_like(query)], axis=1)
        rel = starts[pl.ds(t, 1), :] - base - first
        top = jnp.full((8, TQ), FAR, F32)
        for k, n in CHUNKS:
            s = lax.dot_general(
                kq[pl.ds(first + k, n), :], query, (((1,), (1,)), ((), ())), preferred_element_type=F32
            )
            past = lax.broadcasted_iota(jnp.int32, (n, TQ), 0) - (rel - k)
            s = jnp.where(past.astype(jnp.uint32) < jnp.uint32(WIN), s, FAR)
            scores[pl.ds(k, n), :] = s
            top = jnp.maximum(top, jnp.max(s.reshape(n // 8, 8, TQ), axis=0))
        top = jnp.max(top, axis=0, keepdims=True)
        for k, n in CHUNKS:
            probs[t, pl.ds(k, n), :] = jnp.exp2((scores[pl.ds(k, n), :] - top) * fold).astype(BF16)

        @pl.when(t == 1)
        def _():
            for i in far:
                x_copies[i].wait_recv()
                t_copies[i].start()

        @pl.when(t == 4)
        def _():
            for copy in t_copies:
                copy.wait_recv()
            loads[3].wait()
            grad[...] = lax.dot_general(
                cot_ref[...], weight[...], (((1,), (1,)), ((), ())), preferred_element_type=F32
            ).astype(BF16)
            pair_up(*halves(grad), g_send)
            for copy in g_copies:
                copy.start()
            g_recv[place] = g_send[place]

        @pl.when(t == 3)
        def _():
            v_on(place)
            for i in near:
                v_copies[i].wait_recv()
                v_on(lax.rem(place + HEADS - i - 1, HEADS))

    @pl.loop(0, HEADS)
    def _(p):
        lay_values(v_recv[p], pl.multiple_of(RIM + p * points, 16))

    for copy in v_rim_copies:
        copy.wait_recv()

    @pl.loop(0, rim_blocks)
    def _(p):
        lay_values(v_rims[p], pl.multiple_of(p * points, 16))
        lay_values(v_rims[p + rim_blocks], pl.multiple_of(RIM + span + p * points, 16))

    @pl.loop(0, held // 128)
    def _(t):
        turn(pl.multiple_of(t * 128, 128), 128)

    turn(held // 128 * 128, held % 128)

    @pl.loop(0, span // TQ)
    def _(step):
        t = step + back * (tiles - 1 - 2 * step)
        first = pl.multiple_of(t * TQ, TQ)
        made = jnp.dot(values_t[:, pl.ds(first, SPAN)], probs[t], preferred_element_type=F32)
        share = 1.0 / made[HEAD : HEAD + 1]
        shares[pl.ds(t, 1), :] = share
        out_t = made[:HEAD] * share
        outs_t[t] = out_t
        flows[pl.ds(first, TQ), :] = jnp.concatenate([out_t, out_t], axis=0).T.astype(BF16)

        @pl.when(step == tiles // 2 - 1)
        def _():
            for i in range(half_row):
                send_o(back * half_row + lax.rem(place + i, half_row))

    for i in range(half_row):
        send_o((1 - back) * half_row + lax.rem(place + i, half_row))

    for copy in g_copies:
        copy.wait_recv()

    @pl.loop(0, HEADS)
    def _(p):
        b = g_recv[p]
        at = pl.multiple_of(p * points, 16)
        low = kq[pl.ds(pl.multiple_of(at + RIM, 16), side), HEAD:]
        high = kq[pl.ds(pl.multiple_of(at + side + RIM, 16), side), HEAD:]
        qg[pl.ds(at, side), :] = jnp.concatenate([low, b[:, :HEAD]], axis=1)
        qg[pl.ds(at + side, side), :] = jnp.concatenate([high, b[:, HEAD:]], axis=1)

    def dq_copy(p):
        return push(dq_send.at[p], dq_recv.at[place], dq_ss.at[p], dq_rs.at[place], row * HEADS + p)

    def send_dq(p):
        at = pl.multiple_of(p * points, 16)
        low, high = flows[pl.ds(at, side), :], flows[pl.ds(at + side, side), :]
        dq_send[p] = jnp.concatenate([low[:, :HEAD], high[:, HEAD:]], axis=1)

        @pl.when(p != place)
        def _():
            dq_copy(p).start()

        @pl.when(p == place)
        def _():
            dq_recv[p] = dq_send[p]

    def back_copy(p):
        return push(kv_sum.at[block(p)], kv_back.at[place], b_ss.at[p], b_rs.at[place], row * HEADS + p)

    def send_back(p, rim, at):
        value = acc[block(p, RIM), :]
        if rim is not None:
            value += rim_recv[rim, block(at), :].astype(F32)
        kv_sum[block(p), :] = value.astype(BF16)

        @pl.when(p != place)
        def _():
            back_copy(p).start()

        @pl.when(p == place)
        def _():
            kv_back[p] = kv_sum[block(p), :]

    towards = lower + back * (upper - lower)
    away = lower + upper - towards

    def rim_back(i, b):
        slot, device = (back, away) if i else (1 - back, towards)
        at = i * rim_blocks + b
        return push(rim_send.at[i, block(b)], rim_recv.at[slot, block(b)], back_ss.at[at], back_rs.at[at], device)

    rim_backs = [rim_back(i, b) for i in range(2) for b in range(rim_blocks)]

    def send_rim(i, side_of_row):
        for b in range(rim_blocks):
            rim_send[i, block(b), :] = acc[block(b, side_of_row * (RIM + span)), :].astype(BF16)
            rim_back(i, b).start()

    sib_copy = push(terms.at[1 - core], sib_recv, sib_ss, sib_rs, sibling)

    def to_sum(r):
        return pl.ds(pl.multiple_of(r * half, half), half)

    sum_ats = [to_sum(lax.rem(row + i, rows)) for i in range(rows)]
    s_copies = [push(half_sum.at[sum_ats[i + 1]], peer_recv.at[i], s_ss.at[i], s_rs.at[i], peers[i]) for i in far]
    place_in_half = place // 2
    z_goals = [core * (HEADS // 2) + j for j in range(HEADS // 2)]
    z_copies = [
        push(flat.at[pl.ds(j * part, part)], last_recv.at[place_in_half], z_ss.at[j], z_rs.at[place_in_half], row * HEADS + goal)
        for j, goal in enumerate(z_goals)
    ]

    free = rim_blocks

    def send_first(i):
        p = i + back * (HEADS - 1 - 2 * i)
        at = p - back * (HEADS - free)
        rim_back(0, at).wait_recv()
        send_back(p, back, at)

    low_lanes = lanes_low((TQ, 2 * HEAD))

    @pl.loop(0, span // TQ)
    def _(step):
        t = step + back * (tiles - 1 - 2 * step)
        first = pl.multiple_of(t * TQ, TQ)
        query = qg[pl.ds(first, TQ), :]
        wide = query.astype(F32)
        slant = query[:, HEAD:]
        share = shares[pl.ds(t, 1), :]
        delta = jnp.sum(wide.T[HEAD:] * outs_t[t], axis=0, keepdims=True)
        scaled = wide * jnp.broadcast_to(share, (2 * HEAD, TQ)).T
        for_keys = jnp.where(low_lanes, scaled * scale, 0.0).astype(BF16)
        for_values = jnp.where(low_lanes, 0.0, scaled).astype(BF16)
        dq_t = jnp.zeros((HEAD, TQ), F32)
        for k, n in LONG_CHUNKS:
            turned = lax.dot_general(
                vals[pl.ds(first + k, n), :], slant, (((1,), (1,)), ((), ())), preferred_element_type=F32
            )
            p = probs[t, pl.ds(k, n), :]
            ds = p * (turned - delta).astype(BF16)
            dq_t += jnp.dot(keys_t[:, pl.ds(first + k, n)], ds, preferred_element_type=F32)
            acc[pl.ds(first + k, n), :] += jnp.dot(ds, for_keys, preferred_element_type=F32) + jnp.dot(
                p, for_values, preferred_element_type=F32
            )
        dq_t = dq_t * (share * scale)
        flows[pl.ds(first, TQ), :] = jnp.concatenate([dq_t, dq_t], axis=0).T.astype(BF16)

        @pl.when(step == 5)
        def _():
            for p in range(HEADS):

                @pl.when(p != place)
                def _():
                    push(o_send.at[p], o_recv.at[p], o_ss.at[p], o_rs.at[p], row * HEADS + p).wait_recv()

            split_up(o_recv, *halves(mixed))
            for k in range(HEADS // 2):
                term = lax.dot_general(
                    mixed[:, pl.ds(2 * HEAD * k, 2 * HEAD)], cot_ref[...], (((0,), (0,)), ((), ())),
                    preferred_element_type=F32,
                ).astype(BF16)
                for j in range(4):
                    terms[j % 2, pl.ds((2 * k + j // 2) * half, half), :] = term[j * half : (j + 1) * half]
            sib_copy.start()
            out_ref[...] = jnp.dot(mixed[...], weight[...], preferred_element_type=F32).astype(BF16)

        @pl.when(step == 8)
        def _():
            sib_copy.wait_recv()
            for i in range(rows):
                at = sum_ats[i]
                half_sum[at, :] = (terms[core, at, :].astype(F32) + sib_recv[at, :].astype(F32)).astype(BF16)

        @pl.when(step == 4)
        def _():
            send_rim(0, back)
            for i in range(half_row):
                send_dq(back * half_row + lax.rem(place + i, half_row))

        @pl.when(step == 7)
        def _():
            for i in range(5):
                send_first(lax.rem(place + i, 5))

        @pl.when(step == 8)
        def _():
            for i in range(2):
                send_first(5 + lax.rem(place + i, 2))

    send_rim(1, 1 - back)
    for i in range(half_row):
        send_dq((1 - back) * half_row + lax.rem(place + i, half_row))
    for i in range(HEADS - 2 * free):
        send_back(free + i, None, None)
    for copy in s_copies:
        copy.start()
    for i in range(free):
        at = lax.rem(place + i, free)
        rim_back(1, at).wait_recv()
        send_back((1 - back) * (HEADS - free) + at, 1 - back, at)

    total = half_sum[sum_ats[0], :].astype(F32)
    for i in far:
        s_copies[i].wait_recv()
        total += peer_recv[i].astype(F32)
    total = total * inverse_root
    for b in range(D // 128):
        flat[pl.ds(b, half, stride=D // 128), :] = total[:, b * 128 : (b + 1) * 128]
    for j, goal in enumerate(z_goals):

        @pl.when(goal != place)
        def _():
            z_copies[j].start()

        @pl.when(goal == place)
        def _():
            last_recv[place_in_half] = flat[pl.ds(j * part, part), :]

    for z in range(HEADS // 2):
        source = 2 * z + place // (HEADS // 2)

        @pl.when(source != place)
        def _():
            push(flat.at[pl.ds(0, part)], last_recv.at[z], z_ss.at[0], z_rs.at[z], row * HEADS + source).wait_recv()

    dw_ref[...] = jnp.sum(last_recv[...], axis=0)

    for p in range(HEADS):

        @pl.when(p != place)
        def _():
            push(dq_send.at[p], dq_recv.at[p], dq_ss.at[p], dq_rs.at[p], row * HEADS + p).wait_recv()
            push(kv_sum.at[block(p)], kv_back.at[p], b_ss.at[p], b_rs.at[p], row * HEADS + p).wait_recv()
            dq_copy(p).wait_send()
            o_copy(p).wait_send()
            back_copy(p).wait_send()

    for goal, copy in zip(z_goals, z_copies, strict=True):

        @pl.when(goal != place)
        def _():
            copy.wait_send()

    for copies in (
        w_copies, kv_copies, st_copies, v_copies, x_copies, t_copies, rim_copies, v_rim_copies, g_copies,
        rim_backs, [sib_copy], s_copies,
    ):
        for copy in copies:
            copy.wait_send()


def unpack_kernel(out_in, dq_in, kv_in, dw_in, out_ref, dq_ref, dk_ref, dv_ref, dw_ref):
    out_ref[...] = out_in[...]
    dw_ref[...] = dw_in[...]
    split_up(dq_in, *halves(dq_ref))
    split_up(kv_in, dk_ref, dv_ref)


def in_vmem(count):
    return [pl.BlockSpec(memory_space=pltpu.VMEM)] * count


def anywhere(count):
    return [pl.BlockSpec(memory_space=pl.ANY)] * count


def per_device(queries, key_rows, value_rows, out_weight, cotangent, row_lengths, window_shift):
    points = queries.shape[0]
    devices = lax.axis_size("seq")
    rows = devices // HEADS
    span = HEADS * points
    held = span + 2 * RIM
    tiles = span // TQ
    lanes = -(-held // 128) * 128
    w_part = out_weight.shape[0] // 128
    wide = 2 * HEAD
    half = HEAD // 2
    dma = pltpu.SemaphoreType.DMA
    ring, all_row, cross = dma((HEADS - 1,)), dma((HEADS,)), dma((rows - 1,))
    full = jax.ShapeDtypeStruct((points, D), BF16)
    own = pltpu.VMEM((points, D), BF16)
    sums = jax.ShapeDtypeStruct((w_part, 128), F32)
    blocks = pltpu.VMEM((HEADS, points, wide), BF16)
    packed = pltpu.VMEM((HEADS, points // 2, wide), BF16)
    made = pl.pallas_call(
        functools.partial(layer_kernel, rows, 1.0 / math.sqrt(devices * points)),
        out_shape=(
            full,
            jax.ShapeDtypeStruct((HEADS, points // 2, wide), BF16),
            jax.ShapeDtypeStruct((HEADS, points, wide), BF16),
            sums,
        ),
        in_specs=anywhere(4) + in_vmem(3),
        out_specs=tuple(in_vmem(4)),
        scratch_shapes=[
            own, own, own, own,
            blocks, packed, packed, packed, packed, packed, packed, packed,
            pltpu.VMEM((2 * RIM // points, points // 2, wide), BF16),
            pltpu.VMEM((held, wide), BF16),
            pltpu.VMEM((held, HEAD), BF16),
            pltpu.VMEM((span, wide), BF16),
            pltpu.VMEM((8, 256), jnp.int32),
            pltpu.VMEM((HEADS, 8, 256), jnp.int32),
            pltpu.VMEM((tiles, TQ), jnp.int32),
            pltpu.VMEM((HEADS * w_part, 128), BF16),
            pltpu.VMEM((HEADS * w_part, 128), F32),
            pltpu.VMEM((D, D), BF16),
            pltpu.VMEM((points, D), BF16),
            pltpu.VMEM((HEAD, lanes), BF16),
            pltpu.VMEM((HEAD + 16, lanes), BF16),
            pltpu.VMEM((held, wide), F32),
            pltpu.VMEM((SPAN, TQ), F32),
            pltpu.VMEM((tiles, SPAN, TQ), BF16),
            pltpu.VMEM((tiles, HEAD, TQ), F32),
            pltpu.VMEM((tiles, TQ), F32),
            pltpu.VMEM((span, wide), BF16),
            pltpu.VMEM((points, D), BF16),
            pltpu.VMEM((2, rows * half, D), BF16),
            pltpu.VMEM((rows * half, D), BF16),
            pltpu.VMEM((rows * half, D), BF16),
            pltpu.VMEM((rows - 1, half, D), BF16),
            pltpu.VMEM((half * D // 128, 128), F32),
            pltpu.VMEM((HEADS // 2, w_part, 128), F32),
            pltpu.VMEM((2, RIM, wide), BF16),
            pltpu.VMEM((2, RIM, wide), BF16),
            pltpu.VMEM((span, wide), BF16),
            dma((4,)),
            ring, ring, ring, ring, ring, ring, all_row, all_row, ring, ring, ring, ring,
            all_row, all_row, all_row, all_row, cross, cross, cross, cross, cross, cross,
            all_row, all_row, all_row, all_row, dma((2 * (RIM // points),)), dma((2 * (RIM // points),)), dma, dma,
            dma((HEADS // 2,)), dma((HEADS // 2,)),
        ],
        compiler_params=pltpu.CompilerParams(
            collective_id=0, has_side_effects=True, vmem_limit_bytes=VMEM_LIMIT
        ),
        name="layer",
    )(
        queries, key_rows, value_rows, cotangent, out_weight.reshape(w_part, 128),
        row_lengths.reshape(1, -1), window_shift.reshape(1, -1),
    )
    out, dq, dk, dv, dw = pl.pallas_call(
        unpack_kernel,
        out_shape=(full, full, full, full, sums),
        in_specs=in_vmem(4),
        out_specs=tuple(in_vmem(5)),
        compiler_params=pltpu.CompilerParams(vmem_limit_bytes=VMEM_LIMIT),
        name="unpack",
    )(*made)
    return (out, dq, dk, dv, dw.reshape(-1))


def solution(mesh):
    whole = P("seq", None)
    return jax.shard_map(
        per_device,
        mesh=mesh,
        in_specs=(whole, whole, whole, P("seq"), whole, P(), P("seq")),
        out_specs=(whole, whole, whole, whole, P("seq")),
        check_vma=False,
    )
```

```python
import functools
import math

import jax
import jax.numpy as jnp
from jax import lax
from jax.experimental import pallas as pl
from jax.experimental.pallas import tpu as pltpu
from jax.sharding import PartitionSpec as P

D = 1024
HEADS = 16
HEAD = 64
WIN = 1120
RIM = 1120
TQ = 256
SPAN = 2496
CHUNKS = [(k, min(256, SPAN - k)) for k in range(0, SPAN, 256)]
LONG_CHUNKS = [(k, min(1280, SPAN - k)) for k in range(0, SPAN, 1280)]
FAR = -1e30
MESH = pl.DeviceIdType.MESH
BF16 = jnp.bfloat16
F32 = jnp.float32
VMEM_LIMIT = 56 * 1024 * 1024


def spot():
    me = lax.axis_index("seq")
    return me, me // HEADS, lax.rem(me, HEADS)


def push(src, dst, send, recv, device):
    return pltpu.make_async_remote_copy(
        src_ref=src, dst_ref=dst, send_sem=send, recv_sem=recv, device_id=(device,), device_id_type=MESH
    )


def lanes_low(shape):
    return lax.broadcasted_iota(jnp.int32, shape, 1) < HEAD


def pair_up(left, right, out):
    for k in range(HEADS // 2):
        cols = pl.ds(2 * HEAD * k, 2 * HEAD)
        a, b = left[:, cols], right[:, cols]
        out[2 * k] = jnp.concatenate([a[:, :HEAD], b[:, :HEAD]], axis=1)
        out[2 * k + 1] = jnp.concatenate([a[:, HEAD:], b[:, HEAD:]], axis=1)


def split_up(blocks, left, right):
    for k in range(HEADS // 2):
        cols = pl.ds(2 * HEAD * k, 2 * HEAD)
        a, b = blocks[2 * k], blocks[2 * k + 1]
        left[:, cols] = jnp.concatenate([a[:, :HEAD], b[:, :HEAD]], axis=1)
        right[:, cols] = jnp.concatenate([a[:, HEAD:], b[:, HEAD:]], axis=1)


def halves(ref):
    half = ref.shape[0] // 2
    return ref.at[pl.ds(0, half)], ref.at[pl.ds(half, half)]


def own_starts(len_ref, shift_ref, first_point, offset, all_points):
    count, points = len_ref.shape[1], shift_ref.shape[1]
    lens = jnp.concatenate([len_ref[...], jnp.zeros((1, 256 - count), jnp.int32)], axis=1)
    order = lax.broadcasted_iota(jnp.int32, (256, 256), 0)
    column = lax.broadcasted_iota(jnp.int32, (256, 256), 1)
    ends = jnp.sum(jnp.where(column <= order, lens, 0).astype(F32), axis=1, keepdims=True).astype(jnp.int32)
    lane = lax.broadcasted_iota(jnp.int32, (256, 256), 1)
    index = first_point + lane
    past = (ends <= index) & (order < count)
    row_first = jnp.max(jnp.where(past, jnp.broadcast_to(ends, (256, 256)), 0).astype(F32), axis=0, keepdims=True).astype(jnp.int32)
    shift = jnp.concatenate([shift_ref[...], jnp.zeros((1, 256 - points), jnp.int32)], axis=1)
    starts = jnp.clip(row_first - shift, 0, all_points - WIN)
    starts = jnp.where(lane[:1] < points, starts, 0)
    return pltpu.roll(jnp.broadcast_to(starts, (8, 256)), offset, 1)


def layer_kernel(
    rows, inverse_root,
    q_in, k_in, v_in, cot_in, w_ref, len_ref, shift_ref,
    out_ref, dq_recv, kv_back, dw_ref,
    q_ref, k_ref, v_ref, cot_ref,
    kq_send, v_send, v_recv, g_send, g_recv, o_send, o_recv, dq_send,
    v_rims, kq, vals, qg, st_send, st_recv, starts, w_recv, w_wide, weight, grad,
    keys_t, values_t, acc, scores, probs, outs_t, shares, flows,
    mixed, terms, sib_recv, half_sum, peer_recv, flat, last_recv,
    rim_send, rim_recv, kv_sum,
    in_sems,
    kv_ss, kv_rs, v_ss, v_rs, g_ss, g_rs, o_ss, o_rs, st_ss, st_rs, w_ss, w_rs,
    dq_ss, dq_rs, b_ss, b_rs, x_ss, x_rs, s_ss, s_rs, t_ss, t_rs, rim_ss, rim_rs, vr_ss, vr_rs, back_ss, back_rs, sib_ss, sib_rs,
    z_ss, z_rs,
):
    me, row, place = spot()
    core = lax.rem(me, 2)
    back = lax.rem(core + row, 2)
    points = q_ref.shape[0]
    span = HEADS * points
    held = kq.shape[0]
    scale = 1.0 / math.sqrt(HEAD)
    fold = scale * math.log2(math.e)
    sibling = me + 1 - 2 * core
    near = range(HEADS - 1)
    far = range(rows - 1)
    goals = [lax.rem(place + i, HEADS) for i in range(1, HEADS)]
    mates = [row * HEADS + goal for goal in goals]
    peers = [lax.rem(row + i, rows) * HEADS + place for i in range(1, rows)]
    lower = lax.rem(row + rows - 1, rows) * HEADS + place
    upper = lax.rem(row + 1, rows) * HEADS + place

    def block(at, offset=0):
        return pl.ds(pl.multiple_of(offset + at * points, 16), points)

    barrier = pltpu.get_barrier_semaphore()
    for device in mates + peers:
        pl.semaphore_signal(barrier, inc=1, device_id=(device,), device_id_type=MESH)
    loads = [
        pltpu.make_async_copy(src, dst, in_sems.at[i])
        for i, (src, dst) in enumerate(((k_in, k_ref), (q_in, q_ref), (v_in, v_ref), (cot_in, cot_ref)))
    ]
    for copy in loads:
        copy.start()
    loads[0].wait()
    loads[1].wait()
    pair_up(k_ref, q_ref, kq_send)
    pl.semaphore_wait(barrier, len(mates) + len(peers))

    part = w_ref.shape[0]
    w_at = pl.ds(pl.multiple_of(place * part, part), part)
    w_copies = [push(w_ref, w_recv.at[w_at], w_ss.at[i], w_rs.at[i], mates[i]) for i in near]
    kv_copies = [push(kq_send.at[goals[i]], kq.at[block(place, RIM)], kv_ss.at[i], kv_rs.at[i], mates[i]) for i in near]
    v_copies = [push(v_send.at[goals[i]], v_recv.at[place], v_ss.at[i], v_rs.at[i], mates[i]) for i in near]
    st_copies = [push(st_send, st_recv.at[place], st_ss.at[i], st_rs.at[i], mates[i]) for i in near]
    for copy in kv_copies + w_copies:
        copy.start()
    loads[2].wait()
    pair_up(*halves(v_ref), v_send)
    for copy in v_copies:
        copy.start()
    st_send[...] = own_starts(
        len_ref, shift_ref, me * points, lax.rem(place * points, 128), rows * span
    )
    for copy in st_copies:
        copy.start()
    w_recv[w_at] = w_ref[...]
    kq[block(place, RIM), :] = kq_send[place]
    v_recv[place] = v_send[place]
    st_recv[place] = st_send[...]

    for copy in w_copies:
        copy.wait_recv()
    w_wide[...] = w_recv[...].astype(F32)
    wrows = HEADS * part * 2 * HEAD // D
    half = wrows // 2
    own = pl.multiple_of(row * wrows, 16)
    for b in range(D // 128):
        weight[pl.ds(own, wrows), pl.ds(b * 128, 128)] = w_wide[pl.ds(b, wrows, stride=D // 128), :].astype(BF16)
    my_half = weight.at[pl.ds(pl.multiple_of(own + core * half, 16), half)]
    x_copies = [push(my_half, my_half, x_ss.at[i], x_rs.at[i], peers[i]) for i in far]
    for copy in x_copies:
        copy.start()

    @pl.loop(0, held // 160)
    def _(t):
        acc[pl.ds(pl.multiple_of(t * 160, 160), 160), :] = jnp.zeros((160, 2 * HEAD), F32)

    values_t[HEAD:, :] = jnp.ones((16, values_t.shape[1]), BF16)

    rim_blocks = RIM // points

    def rim_down(p):
        return push(kq.at[block(p, RIM)], kq.at[block(p, RIM + span)], rim_ss.at[p], rim_rs.at[p], lower)

    def rim_up(p):
        at = p - (HEADS - rim_blocks)
        return push(kq.at[block(p, RIM)], kq.at[block(at)], rim_ss.at[p], rim_rs.at[p], upper)

    def rim_on(p):
        @pl.when(p < rim_blocks)
        def _():
            rim_down(p).start()

        @pl.when(p >= HEADS - rim_blocks)
        def _():
            rim_up(p).start()

    rim_on(place)
    for i in near:
        kv_copies[i].wait_recv()
        rim_on(lax.rem(place + HEADS - i - 1, HEADS))
    rim_copies = [rim_down(p) for p in range(rim_blocks)] + [rim_up(p) for p in range(HEADS - rim_blocks, HEADS)]

    side = points // 2

    def v_down(p):
        return push(v_recv.at[p], v_rims.at[p + rim_blocks], vr_ss.at[p], vr_rs.at[p], lower)

    def v_up(p):
        return push(v_recv.at[p], v_rims.at[p - (HEADS - rim_blocks)], vr_ss.at[p], vr_rs.at[p], upper)

    def v_on(p):
        @pl.when(p < rim_blocks)
        def _():
            v_down(p).start()

        @pl.when(p >= HEADS - rim_blocks)
        def _():
            v_up(p).start()

    v_rim_copies = [v_down(p) for p in range(rim_blocks)] + [v_up(p) for p in range(HEADS - rim_blocks, HEADS)]

    def lay_values(packed, at):
        vals[pl.ds(at, side), :] = packed[:, :HEAD]
        vals[pl.ds(at + side, side), :] = packed[:, HEAD:]

    def turn(at, size):
        keys_t[:, pl.ds(at, size)] = kq[pl.ds(at, size), :].astype(F32).T[:HEAD].astype(BF16)
        values_t[:HEAD, pl.ds(at, size)] = vals[pl.ds(at, size), :].astype(F32).T.astype(BF16)

    sources = [lax.rem(row + rows - i - 1, rows) for i in far]
    came = [weight.at[pl.ds(pl.multiple_of(r * wrows + core * half, 16), half)] for r in sources]
    t_copies = [push(came[i], came[i], t_ss.at[i], t_rs.at[i], sibling) for i in far]
    g_copies = [push(g_send.at[goals[i]], g_recv.at[place], g_ss.at[i], g_rs.at[i], mates[i]) for i in near]

    for copy in st_copies:
        copy.wait_recv()
    for t in range(span // 128):
        total = None
        for p in range(HEADS):
            first = p * points // 128
            if first <= t <= first + 1:
                piece = st_recv[p, 0:1, pl.ds((t - first) * 128, 128)]
                total = piece if total is None else total + piece
        starts[t // 2 : t // 2 + 1, (t % 2) * 128 : (t % 2 + 1) * 128] = total
    for copy in rim_copies:
        copy.wait_recv()

    base = row * span - RIM
    tiles = span // TQ
    half_row = HEADS // 2

    def o_copy(p):
        return push(o_send.at[p], o_recv.at[place], o_ss.at[p], o_rs.at[place], row * HEADS + p)

    def send_o(p):
        at = pl.multiple_of(p * points, 16)
        low, high = flows[pl.ds(at, side), :], flows[pl.ds(at + side, side), :]
        o_send[p] = jnp.concatenate([low[:, :HEAD], high[:, HEAD:]], axis=1)

        @pl.when(p != place)
        def _():
            o_copy(p).start()

        @pl.when(p == place)
        def _():
            o_recv[p] = o_send[p]

    @pl.loop(0, span // TQ)
    def _(t):
        first = pl.multiple_of(t * TQ, TQ)
        query = kq[pl.ds(pl.multiple_of(first + RIM, 16), TQ), HEAD:]
        query = jnp.concatenate([query, jnp.zeros_like(query)], axis=1)
        rel = starts[pl.ds(t, 1), :] - base - first
        top = jnp.full((8, TQ), FAR, F32)
        for k, n in CHUNKS:
            s = lax.dot_general(
                kq[pl.ds(first + k, n), :], query, (((1,), (1,)), ((), ())), preferred_element_type=F32
            )
            past = lax.broadcasted_iota(jnp.int32, (n, TQ), 0) - (rel - k)
            s = jnp.where(past.astype(jnp.uint32) < jnp.uint32(WIN), s, FAR)
            scores[pl.ds(k, n), :] = s
            top = jnp.maximum(top, jnp.max(s.reshape(n // 8, 8, TQ), axis=0))
        top = jnp.max(top, axis=0, keepdims=True)
        for k, n in CHUNKS:
            probs[t, pl.ds(k, n), :] = jnp.exp2((scores[pl.ds(k, n), :] - top) * fold).astype(BF16)

        @pl.when(t == 1)
        def _():
            for i in far:
                x_copies[i].wait_recv()
                t_copies[i].start()

        @pl.when(t == 4)
        def _():
            for copy in t_copies:
                copy.wait_recv()
            loads[3].wait()
            grad[...] = lax.dot_general(
                cot_ref[...], weight[...], (((1,), (1,)), ((), ())), preferred_element_type=F32
            ).astype(BF16)
            pair_up(*halves(grad), g_send)
            for copy in g_copies:
                copy.start()
            g_recv[place] = g_send[place]

        @pl.when(t == 3)
        def _():
            v_on(place)
            for i in near:
                v_copies[i].wait_recv()
                v_on(lax.rem(place + HEADS - i - 1, HEADS))

    @pl.loop(0, HEADS)
    def _(p):
        lay_values(v_recv[p], pl.multiple_of(RIM + p * points, 16))

    for copy in v_rim_copies:
        copy.wait_recv()

    @pl.loop(0, rim_blocks)
    def _(p):
        lay_values(v_rims[p], pl.multiple_of(p * points, 16))
        lay_values(v_rims[p + rim_blocks], pl.multiple_of(RIM + span + p * points, 16))

    @pl.loop(0, held // 128)
    def _(t):
        turn(pl.multiple_of(t * 128, 128), 128)

    turn(held // 128 * 128, held % 128)

    @pl.loop(0, span // TQ)
    def _(step):
        t = step + back * (tiles - 1 - 2 * step)
        first = pl.multiple_of(t * TQ, TQ)
        made = jnp.dot(values_t[:, pl.ds(first, SPAN)], probs[t], preferred_element_type=F32)
        share = 1.0 / made[HEAD : HEAD + 1]
        shares[pl.ds(t, 1), :] = share
        out_t = made[:HEAD] * share
        outs_t[t] = out_t
        flows[pl.ds(first, TQ), :] = jnp.concatenate([out_t, out_t], axis=0).T.astype(BF16)

        @pl.when(step == tiles // 2 - 1)
        def _():
            for i in range(half_row):
                send_o(back * half_row + lax.rem(place + i, half_row))

    for i in range(half_row):
        send_o((1 - back) * half_row + lax.rem(place + i, half_row))

    for copy in g_copies:
        copy.wait_recv()

    @pl.loop(0, HEADS)
    def _(p):
        b = g_recv[p]
        at = pl.multiple_of(p * points, 16)
        low = kq[pl.ds(pl.multiple_of(at + RIM, 16), side), HEAD:]
        high = kq[pl.ds(pl.multiple_of(at + side + RIM, 16), side), HEAD:]
        qg[pl.ds(at, side), :] = jnp.concatenate([low, b[:, :HEAD]], axis=1)
        qg[pl.ds(at + side, side), :] = jnp.concatenate([high, b[:, HEAD:]], axis=1)

    def dq_copy(p):
        return push(dq_send.at[p], dq_recv.at[place], dq_ss.at[p], dq_rs.at[place], row * HEADS + p)

    def send_dq(p):
        at = pl.multiple_of(p * points, 16)
        low, high = flows[pl.ds(at, side), :], flows[pl.ds(at + side, side), :]
        dq_send[p] = jnp.concatenate([low[:, :HEAD], high[:, HEAD:]], axis=1)

        @pl.when(p != place)
        def _():
            dq_copy(p).start()

        @pl.when(p == place)
        def _():
            dq_recv[p] = dq_send[p]

    def back_copy(p):
        return push(kv_sum.at[block(p)], kv_back.at[place], b_ss.at[p], b_rs.at[place], row * HEADS + p)

    def send_back(p, rim, at):
        value = acc[block(p, RIM), :]
        if rim is not None:
            value += rim_recv[rim, block(at), :].astype(F32)
        kv_sum[block(p), :] = value.astype(BF16)

        @pl.when(p != place)
        def _():
            back_copy(p).start()

        @pl.when(p == place)
        def _():
            kv_back[p] = kv_sum[block(p), :]

    towards = lower + back * (upper - lower)
    away = lower + upper - towards

    def rim_back(i, b):
        slot, device = (back, away) if i else (1 - back, towards)
        at = i * rim_blocks + b
        return push(rim_send.at[i, block(b)], rim_recv.at[slot, block(b)], back_ss.at[at], back_rs.at[at], device)

    rim_backs = [rim_back(i, b) for i in range(2) for b in range(rim_blocks)]

    def send_rim(i, side_of_row):
        for b in range(rim_blocks):
            rim_send[i, block(b), :] = acc[block(b, side_of_row * (RIM + span)), :].astype(BF16)
            rim_back(i, b).start()

    sib_copy = push(terms.at[1 - core], sib_recv, sib_ss, sib_rs, sibling)

    def to_sum(r):
        return pl.ds(pl.multiple_of(r * half, half), half)

    sum_ats = [to_sum(lax.rem(row + i, rows)) for i in range(rows)]
    s_copies = [push(half_sum.at[sum_ats[i + 1]], peer_recv.at[i], s_ss.at[i], s_rs.at[i], peers[i]) for i in far]
    place_in_half = place // 2
    z_goals = [core * (HEADS // 2) + j for j in range(HEADS // 2)]
    z_copies = [
        push(flat.at[pl.ds(j * part, part)], last_recv.at[place_in_half], z_ss.at[j], z_rs.at[place_in_half], row * HEADS + goal)
        for j, goal in enumerate(z_goals)
    ]

    free = rim_blocks

    def send_first(i):
        p = i + back * (HEADS - 1 - 2 * i)
        at = p - back * (HEADS - free)
        rim_back(0, at).wait_recv()
        send_back(p, back, at)

    low_lanes = lanes_low((TQ, 2 * HEAD))

    @pl.loop(0, span // TQ)
    def _(step):
        t = step + back * (tiles - 1 - 2 * step)
        first = pl.multiple_of(t * TQ, TQ)
        query = qg[pl.ds(first, TQ), :]
        wide = query.astype(F32)
        slant = query[:, HEAD:]
        share = shares[pl.ds(t, 1), :]
        delta = jnp.sum(wide.T[HEAD:] * outs_t[t], axis=0, keepdims=True)
        scaled = wide * jnp.broadcast_to(share, (2 * HEAD, TQ)).T
        for_keys = jnp.where(low_lanes, scaled * scale, 0.0).astype(BF16)
        for_values = jnp.where(low_lanes, 0.0, scaled).astype(BF16)
        dq_t = jnp.zeros((HEAD, TQ), F32)
        for k, n in LONG_CHUNKS:
            turned = lax.dot_general(
                vals[pl.ds(first + k, n), :], slant, (((1,), (1,)), ((), ())), preferred_element_type=F32
            )
            p = probs[t, pl.ds(k, n), :]
            ds = p * (turned - delta).astype(BF16)
            dq_t += jnp.dot(keys_t[:, pl.ds(first + k, n)], ds, preferred_element_type=F32)
            acc[pl.ds(first + k, n), :] += jnp.dot(ds, for_keys, preferred_element_type=F32) + jnp.dot(
                p, for_values, preferred_element_type=F32
            )
        dq_t = dq_t * (share * scale)
        flows[pl.ds(first, TQ), :] = jnp.concatenate([dq_t, dq_t], axis=0).T.astype(BF16)

        @pl.when(step == 5)
        def _():
            for p in range(HEADS):

                @pl.when(p != place)
                def _():
                    push(o_send.at[p], o_recv.at[p], o_ss.at[p], o_rs.at[p], row * HEADS + p).wait_recv()

            split_up(o_recv, *halves(mixed))
            for k in range(HEADS // 2):
                term = lax.dot_general(
                    mixed[:, pl.ds(2 * HEAD * k, 2 * HEAD)], cot_ref[...], (((0,), (0,)), ((), ())),
                    preferred_element_type=F32,
                ).astype(BF16)
                for j in range(4):
                    terms[j % 2, pl.ds((2 * k + j // 2) * half, half), :] = term[j * half : (j + 1) * half]
            sib_copy.start()
            out_ref[...] = jnp.dot(mixed[...], weight[...], preferred_element_type=F32).astype(BF16)

        @pl.when(step == 8)
        def _():
            sib_copy.wait_recv()
            for i in range(rows):
                at = sum_ats[i]
                half_sum[at, :] = (terms[core, at, :].astype(F32) + sib_recv[at, :].astype(F32)).astype(BF16)

        @pl.when(step == 4)
        def _():
            send_rim(0, back)
            for i in range(half_row):
                send_dq(back * half_row + lax.rem(place + i, half_row))

        @pl.when(step == 7)
        def _():
            for i in range(5):
                send_first(lax.rem(place + i, 5))

        @pl.when(step == 8)
        def _():
            for i in range(2):
                send_first(5 + lax.rem(place + i, 2))

    send_rim(1, 1 - back)
    for i in range(half_row):
        send_dq((1 - back) * half_row + lax.rem(place + i, half_row))
    for i in range(HEADS - 2 * free):
        send_back(free + i, None, None)
    for copy in s_copies:
        copy.start()
    for i in range(free):
        at = lax.rem(place + i, free)
        rim_back(1, at).wait_recv()
        send_back((1 - back) * (HEADS - free) + at, 1 - back, at)

    total = half_sum[sum_ats[0], :].astype(F32)
    for i in far:
        s_copies[i].wait_recv()
        total += peer_recv[i].astype(F32)
    total = total * inverse_root
    for b in range(D // 128):
        flat[pl.ds(b, half, stride=D // 128), :] = total[:, b * 128 : (b + 1) * 128]
    for j, goal in enumerate(z_goals):

        @pl.when(goal != place)
        def _():
            z_copies[j].start()

        @pl.when(goal == place)
        def _():
            last_recv[place_in_half] = flat[pl.ds(j * part, part), :]

    for z in range(HEADS // 2):
        source = 2 * z + place // (HEADS // 2)

        @pl.when(source != place)
        def _():
            push(flat.at[pl.ds(0, part)], last_recv.at[z], z_ss.at[0], z_rs.at[z], row * HEADS + source).wait_recv()

    dw_ref[...] = jnp.sum(last_recv[...], axis=0)

    for p in range(HEADS):

        @pl.when(p != place)
        def _():
            push(dq_send.at[p], dq_recv.at[p], dq_ss.at[p], dq_rs.at[p], row * HEADS + p).wait_recv()
            push(kv_sum.at[block(p)], kv_back.at[p], b_ss.at[p], b_rs.at[p], row * HEADS + p).wait_recv()
            dq_copy(p).wait_send()
            o_copy(p).wait_send()
            back_copy(p).wait_send()

    for goal, copy in zip(z_goals, z_copies, strict=True):

        @pl.when(goal != place)
        def _():
            copy.wait_send()

    for copies in (
        w_copies, kv_copies, st_copies, v_copies, x_copies, t_copies, rim_copies, v_rim_copies, g_copies,
        rim_backs, [sib_copy], s_copies,
    ):
        for copy in copies:
            copy.wait_send()


def unpack_kernel(out_in, dq_in, kv_in, dw_in, out_ref, dq_ref, dk_ref, dv_ref, dw_ref):
    out_ref[...] = out_in[...]
    dw_ref[...] = dw_in[...]
    split_up(dq_in, *halves(dq_ref))
    split_up(kv_in, dk_ref, dv_ref)


def in_vmem(count):
    return [pl.BlockSpec(memory_space=pltpu.VMEM)] * count


def anywhere(count):
    return [pl.BlockSpec(memory_space=pl.ANY)] * count


def per_device(queries, key_rows, value_rows, out_weight, cotangent, row_lengths, window_shift):
    points = queries.shape[0]
    devices = lax.axis_size("seq")
    rows = devices // HEADS
    span = HEADS * points
    held = span + 2 * RIM
    tiles = span // TQ
    lanes = -(-held // 128) * 128
    w_part = out_weight.shape[0] // 128
    wide = 2 * HEAD
    half = HEAD // 2
    dma = pltpu.SemaphoreType.DMA
    ring, all_row, cross = dma((HEADS - 1,)), dma((HEADS,)), dma((rows - 1,))
    full = jax.ShapeDtypeStruct((points, D), BF16)
    own = pltpu.VMEM((points, D), BF16)
    sums = jax.ShapeDtypeStruct((w_part, 128), F32)
    blocks = pltpu.VMEM((HEADS, points, wide), BF16)
    packed = pltpu.VMEM((HEADS, points // 2, wide), BF16)
    made = pl.pallas_call(
        functools.partial(layer_kernel, rows, 1.0 / math.sqrt(devices * points)),
        out_shape=(
            full,
            jax.ShapeDtypeStruct((HEADS, points // 2, wide), BF16),
            jax.ShapeDtypeStruct((HEADS, points, wide), BF16),
            sums,
        ),
        in_specs=anywhere(4) + in_vmem(3),
        out_specs=tuple(in_vmem(4)),
        scratch_shapes=[
            own, own, own, own,
            blocks, packed, packed, packed, packed, packed, packed, packed,
            pltpu.VMEM((2 * RIM // points, points // 2, wide), BF16),
            pltpu.VMEM((held, wide), BF16),
            pltpu.VMEM((held, HEAD), BF16),
            pltpu.VMEM((span, wide), BF16),
            pltpu.VMEM((8, 256), jnp.int32),
            pltpu.VMEM((HEADS, 8, 256), jnp.int32),
            pltpu.VMEM((tiles, TQ), jnp.int32),
            pltpu.VMEM((HEADS * w_part, 128), BF16),
            pltpu.VMEM((HEADS * w_part, 128), F32),
            pltpu.VMEM((D, D), BF16),
            pltpu.VMEM((points, D), BF16),
            pltpu.VMEM((HEAD, lanes), BF16),
            pltpu.VMEM((HEAD + 16, lanes), BF16),
            pltpu.VMEM((held, wide), F32),
            pltpu.VMEM((SPAN, TQ), F32),
            pltpu.VMEM((tiles, SPAN, TQ), BF16),
            pltpu.VMEM((tiles, HEAD, TQ), F32),
            pltpu.VMEM((tiles, TQ), F32),
            pltpu.VMEM((span, wide), BF16),
            pltpu.VMEM((points, D), BF16),
            pltpu.VMEM((2, rows * half, D), BF16),
            pltpu.VMEM((rows * half, D), BF16),
            pltpu.VMEM((rows * half, D), BF16),
            pltpu.VMEM((rows - 1, half, D), BF16),
            pltpu.VMEM((half * D // 128, 128), F32),
            pltpu.VMEM((HEADS // 2, w_part, 128), F32),
            pltpu.VMEM((2, RIM, wide), BF16),
            pltpu.VMEM((2, RIM, wide), BF16),
            pltpu.VMEM((span, wide), BF16),
            dma((4,)),
            ring, ring, ring, ring, ring, ring, all_row, all_row, ring, ring, ring, ring,
            all_row, all_row, all_row, all_row, cross, cross, cross, cross, cross, cross,
            all_row, all_row, all_row, all_row, dma((2 * (RIM // points),)), dma((2 * (RIM // points),)), dma, dma,
            dma((HEADS // 2,)), dma((HEADS // 2,)),
        ],
        compiler_params=pltpu.CompilerParams(
            collective_id=0, has_side_effects=True, vmem_limit_bytes=VMEM_LIMIT
        ),
        name="layer",
    )(
        queries, key_rows, value_rows, cotangent, out_weight.reshape(w_part, 128),
        row_lengths.reshape(1, -1), window_shift.reshape(1, -1),
    )
    out, dq, dk, dv, dw = pl.pallas_call(
        unpack_kernel,
        out_shape=(full, full, full, full, sums),
        in_specs=in_vmem(4),
        out_specs=tuple(in_vmem(5)),
        compiler_params=pltpu.CompilerParams(vmem_limit_bytes=VMEM_LIMIT),
        name="unpack",
    )(*made)
    return (out, dq, dk, dv, dw.reshape(-1))


def solution(mesh):
    whole = P("seq", None)
    return jax.shard_map(
        per_device,
        mesh=mesh,
        in_specs=(whole, whole, whole, P("seq"), whole, P(), P("seq")),
        out_specs=(whole, whole, whole, whole, P("seq")),
        check_vma=False,
    )
```
